256 devices in a mesh: seq: 32 (over x, z), col: 8 (over y, core).
Axes of the slice: x: 4, y: 4, z: 8, core: 2. Of those that a mesh axis runs over, the one named last changes fastest.
Arguments:
- embedded_alignment: bfloat16 [256, 512, 768], P('seq', 'col'), may hold values from -5 to 5
- horizontal_input_projections: bfloat16 [768, 2304], replicated, may hold values from -0.29228357 to 0.29228357
- horizontal_final_projection: bfloat16 [768, 768], replicated, may hold values from -0.21875 to 0.21875
- vertical_input_projections: bfloat16 [768, 2304], replicated, may hold values from -0.8660254 to 0.8660254
- vertical_final_projection: bfloat16 [768, 768], replicated, may hold values from -0.21875 to 0.21875
Outputs:
- mixed_msa: bfloat16 [256, 512, 768], P('seq', 'col')
The draws below stay inside these ranges and needn't reach their ends.
All inputs are finite; a program needn't handle non-finite values.
Results may differ from the reference program's by a relative error of at most 0.028.
Values may be sent and summed in bfloat16 or wider, within the bound.
No kernel may reach another device: no remote copies, remote signals or barrier semaphores. Data moves between devices by JAX's collectives and lax.ppermute only.
A program may use at most 128 MiB of HBM per device.

```python
import jax
import jax.numpy as jnp
from jax import lax

D = 768
FOCUS_BRANCHES = 12
SEQS = 256
GLOBAL_SITES = 512


def draw_embedded_alignment(key, part):
    key = jax.random.fold_in(key, 11)
    first = jax.random.fold_in(key, 0)
    return jnp.clip(jax.random.normal(first, (SEQS, GLOBAL_SITES, D), jnp.float32), -5.0, 5.0).astype(jnp.bfloat16)


def draw_horizontal_input_projections(key, part):
    key = jax.random.fold_in(key, 21)
    first, second, third = jax.random.split(key, 3)
    query_part = 2.0 * jnp.clip(jax.random.normal(first, (D, D), jnp.float32), -4.0, 4.0)
    key_part = jnp.clip(jax.random.normal(second, (D, D), jnp.float32), -4.0, 4.0)
    value_part = jnp.clip(jax.random.normal(third, (D, D), jnp.float32), -4.0, 4.0)
    joined = jnp.concatenate([query_part, key_part, value_part], axis=1)
    return (joined * D ** (-0.5)).astype(jnp.bfloat16)


def draw_vertical_input_projections(key, part):
    key = jax.random.fold_in(key, 31)
    first, second, third = jax.random.split(key, 3)
    query_part = 2.0 * jnp.clip(jax.random.normal(first, (D, D), jnp.float32), -4.0, 4.0)
    key_part = jnp.clip(jax.random.normal(second, (D, D), jnp.float32), -4.0, 4.0)
    value_part = jnp.clip(jax.random.normal(third, (D, D), jnp.float32), -4.0, 4.0)
    joined = jnp.concatenate([query_part, key_part, value_part], axis=1)
    return (joined * D ** (-0.5)).astype(jnp.bfloat16)


def gaussian(stream_key, extent, scale, bound, dtype=jnp.bfloat16):
    return jnp.clip(scale * jax.random.normal(stream_key, extent, jnp.float32), -bound, bound).astype(dtype)


def setup_inputs(seed: int = 0) -> dict:
    key_list = jax.random.split(jax.random.key(seed), 6)
    return {
        "embedded_alignment": draw_embedded_alignment(jax.random.fold_in(key_list[5], 71), 0),
        "horizontal_input_projections": draw_horizontal_input_projections(jax.random.fold_in(key_list[5], 71), 0),
        "horizontal_final_projection": gaussian(key_list[2], (D, D), D ** -0.5, 0.21875),
        "vertical_input_projections": draw_vertical_input_projections(jax.random.fold_in(key_list[5], 71), 0),
        "vertical_final_projection": gaussian(key_list[4], (D, D), D ** -0.5, 0.21875),
    }


epsilon = 1e-05

def layer_norm(embedding_entries):
    row_mean = lax.optimization_barrier(jnp.mean(embedding_entries, axis=-1, keepdims=True))
    centered = embedding_entries - row_mean
    spread = lax.optimization_barrier(jnp.mean(centered * centered, axis=-1, keepdims=True))
    return centered * lax.rsqrt(spread + epsilon)

def softmax_last(scores):
    row_maximum = lax.optimization_barrier(jnp.max(scores, axis=-1, keepdims=True))
    powers = jnp.exp(scores - row_maximum)
    return powers / lax.optimization_barrier(jnp.sum(powers, axis=-1, keepdims=True))

def project_rows(sequence, weight):
    normed = layer_norm(sequence.astype(jnp.float32)).astype(jnp.bfloat16)
    return jnp.dot(normed, weight, preferred_element_type=jnp.float32).astype(jnp.bfloat16)

def attend_columns(col_block, vertical_input_projections, vertical_final_projection):
    seq_count, col_count, embedding_entries = col_block.shape
    head_size = embedding_entries // FOCUS_BRANCHES
    normed = layer_norm(col_block.astype(jnp.float32)).astype(jnp.bfloat16)
    projected = jnp.dot(normed.reshape(seq_count * col_count, embedding_entries), vertical_input_projections, preferred_element_type=jnp.float32).astype(jnp.bfloat16)
    projected = projected.reshape(seq_count, col_count, 3, FOCUS_BRANCHES, head_size).astype(jnp.float32)
    queries = projected[:, :, 0]
    key_heads = projected[:, :, 1]
    value_heads = projected[:, :, 2]
    scores = jnp.einsum('rchd,schd->chrs', queries, key_heads) * head_size ** (-0.5)
    weights = softmax_last(scores).astype(jnp.bfloat16).astype(jnp.float32)
    context = jnp.einsum('chrs,schd->rchd', weights, value_heads).astype(jnp.bfloat16)
    update = jnp.dot(context.reshape(seq_count * col_count, embedding_entries), vertical_final_projection, preferred_element_type=jnp.float32)
    return (col_block.astype(jnp.float32) + update.reshape(seq_count, col_count, embedding_entries)).astype(jnp.bfloat16)

def reference(embedded_alignment, horizontal_input_projections, horizontal_final_projection, vertical_input_projections, vertical_final_projection):
    head_size = D // FOCUS_BRANCHES

    def gather_raw_scores(running_sum, sequence):
        projected = project_rows(sequence, horizontal_input_projections)
        queries = projected[:, :D].reshape(GLOBAL_SITES, FOCUS_BRANCHES, head_size).astype(jnp.float32)
        key_heads = projected[:, D:2 * D].reshape(GLOBAL_SITES, FOCUS_BRANCHES, head_size).astype(jnp.float32)
        return (running_sum + jnp.einsum('ihd,jhd->hij', queries, key_heads), None)
    raw_score_grand_addition, discarded_placeholder = lax.scan(gather_raw_scores, jnp.zeros((FOCUS_BRANCHES, GLOBAL_SITES, GLOBAL_SITES), jnp.float32), embedded_alignment)
    weights = softmax_last(raw_score_grand_addition * (head_size * SEQS) ** (-0.5)).astype(jnp.bfloat16)
    weight_wide = weights.astype(jnp.float32)

    def horizontal_blending(sequence):
        projected = project_rows(sequence, horizontal_input_projections)
        value_heads = projected[:, 2 * D:].reshape(GLOBAL_SITES, FOCUS_BRANCHES, head_size).astype(jnp.float32)
        context = jnp.einsum('hij,jhd->ihd', weight_wide, value_heads).reshape(GLOBAL_SITES, D).astype(jnp.bfloat16)
        update = jnp.dot(context, horizontal_final_projection, preferred_element_type=jnp.float32)
        return (sequence.astype(jnp.float32) + update).astype(jnp.bfloat16)
    horizontal_context_result = lax.map(horizontal_blending, embedded_alignment)
    group_size = 8
    grouped = horizontal_context_result.reshape(SEQS, GLOBAL_SITES // group_size, group_size, D).transpose(1, 0, 2, 3)

    def column_group(col_block):
        return attend_columns(col_block, vertical_input_projections, vertical_final_projection)
    finished = lax.map(column_group, grouped)
    return finished.transpose(1, 0, 2, 3).reshape(SEQS, GLOBAL_SITES, D)
```

```python
import functools

import jax
import jax.numpy as jnp
from jax import lax
from jax.experimental import pallas as pl
from jax.experimental.pallas import tpu as pltpu
from jax.sharding import Mesh, PartitionSpec as P

HEADS = 12
PAIRS = 6
D = 768
R = 8
I = 64
EPS = 1e-05
LOG2E = 1.4426950408889634
NT = (((1,), (1,)), ((), ()))
BF = jnp.bfloat16
F32 = jnp.float32
VMEM = pl.BlockSpec(memory_space=pltpu.VMEM)
MB = 1024 * 1024


def params(limit=32 * MB):
    return pltpu.CompilerParams(vmem_limit_bytes=limit)


def cost(flops, bytes_accessed, transcendentals=0):
    return pl.CostEstimate(
        flops=int(flops), bytes_accessed=int(bytes_accessed), transcendentals=int(transcendentals)
    )


def layer_norm(x):
    mean = jnp.mean(x, axis=-1, keepdims=True)
    centered = x - mean
    spread = jnp.mean(centered * centered, axis=-1, keepdims=True)
    return centered * lax.rsqrt(spread + EPS)


def first_head(rows):
    return lax.broadcasted_iota(jnp.int32, (rows, 128), 1) < 64


def query_kernel(x_ref, w_ref, q_ref):
    x = x_ref[...].astype(F32).reshape(2 * I, D)
    normed = layer_norm(x).astype(BF)
    q = jnp.dot(normed, w_ref[...], preferred_element_type=F32).astype(BF)
    first = first_head(I)
    zero = jnp.zeros((I, 128), BF)
    for p in range(PAIRS):
        for r in range(2):
            block = q[r * I : (r + 1) * I, p * 128 : (p + 1) * 128]
            q_ref[p, 0:I, r * 128 : (r + 1) * 128] = jnp.where(first, block, zero)
            q_ref[p, I : 2 * I, r * 128 : (r + 1) * 128] = jnp.where(first, zero, block)


def masked_queries(x, w):
    return pl.pallas_call(
        query_kernel,
        grid=(R // 2,),
        out_shape=jax.ShapeDtypeStruct((PAIRS, 2 * I, R * 128), BF),
        in_specs=[
            pl.BlockSpec((2, I, D), lambda s: (s, 0, 0)),
            pl.BlockSpec((D, D), lambda s: (0, 0)),
        ],
        out_specs=pl.BlockSpec((PAIRS, 2 * I, 256), lambda s: (0, 0, s)),
        compiler_params=params(),
        cost_estimate=cost(2 * R * I * D * D, 4e6),
        name="queries",
    )(x, w)


def pair_kernel(a_ref, b_ref, wk_ref, wv_ref, q_ref, logit_ref, v_ref, acc):
    s = pl.program_id(0)
    rows = []
    for r in range(2):
        rows.append(a_ref[r].astype(F32))
        rows.append(b_ref[r].astype(F32))
    normed = layer_norm(jnp.concatenate(rows, axis=0)).astype(BF)
    k = jnp.dot(normed, wk_ref[...], preferred_element_type=F32).astype(BF)
    for p in range(PAIRS):
        lanes = slice(p * 128, (p + 1) * 128)
        keys = jnp.concatenate([k[0:128, lanes], k[128:256, lanes]], axis=1)
        part = lax.dot_general(q_ref[p], keys, NT, preferred_element_type=F32)

        @pl.when(s == 0)
        def _():
            acc[p] = part

        @pl.when(s > 0)
        def _():
            acc[p] += part

    v = jnp.dot(normed, wv_ref[...], preferred_element_type=F32).astype(BF)
    for p in range(PAIRS):
        lanes = slice(p * 128, (p + 1) * 128)
        v_ref[p, :, 0:128] = v[0:128, lanes]
        v_ref[p, :, 128:256] = v[128:256, lanes]

    @pl.when(s == R // 2 - 1)
    def _():
        logit_ref[...] = acc[...].astype(BF)


def keys_values(a, b, w, q):
    return pl.pallas_call(
        pair_kernel,
        grid=(R // 2,),
        out_shape=(
            jax.ShapeDtypeStruct((PAIRS, 2 * I, 128), BF),
            jax.ShapeDtypeStruct((PAIRS, 128, R * 128), BF),
        ),
        in_specs=[
            pl.BlockSpec((2, I, D), lambda s: (s, 0, 0)),
            pl.BlockSpec((2, I, D), lambda s: (s, 0, 0)),
            pl.BlockSpec((D, D), lambda s: (0, 1)),
            pl.BlockSpec((D, D), lambda s: (0, 2)),
            pl.BlockSpec((PAIRS, 2 * I, 256), lambda s: (0, 0, s)),
        ],
        out_specs=(
            pl.BlockSpec((PAIRS, 2 * I, 128), lambda s: (0, 0, 0)),
            pl.BlockSpec((PAIRS, 128, 256), lambda s: (0, 0, s)),
        ),
        scratch_shapes=[pltpu.VMEM((PAIRS, 2 * I, 128), F32)],
        compiler_params=params(),
        cost_estimate=cost(2 * 1024 * D * 2 * D + 2 * D * 1024 * 128, 8e6),
        name="keys_values",
    )(a, b, w, w, q)


def weight_kernel(scale, copies, *refs):
    out = refs[-1]
    totals = [jnp.sum(ref[...].astype(F32), axis=0) for ref in refs[:-1]]
    logits = jnp.concatenate(totals, axis=1)
    top = jnp.max(logits, axis=-1, keepdims=True)
    powers = jnp.exp2((logits - top) * (scale * LOG2E))
    weights = powers / jnp.sum(powers, axis=-1, keepdims=True)
    weights = weights.astype(BF)
    for c in range(copies):
        out[c] = weights


def row_weights(parts, scale, copies):
    rows = parts[0].shape[1]
    return pl.pallas_call(
        functools.partial(weight_kernel, scale, copies),
        out_shape=jax.ShapeDtypeStruct((copies, rows, 512), BF),
        in_specs=[VMEM] * len(parts),
        out_specs=VMEM,
        compiler_params=params(),
        cost_estimate=cost(1e6, 1.2e6),
        name="row_weights",
    )(*parts)


def reorder(major, minor):
    n = major * minor
    to = lax.broadcasted_iota(jnp.int32, (n, n), 0)
    at = lax.broadcasted_iota(jnp.int32, (n, n), 1)
    source = lax.rem(to, major) * minor + lax.div(to, major)
    return jnp.where(at == source, 1.0, 0.0).astype(BF)


def context_kernel(place_ref, w0, w1, w2, w3, v0, v1, v2, v3, x_ref, wo_ref, first_ref, second_ref, wall, ctx):
    p = pl.program_id(0)

    @pl.when(p == 0)
    def _():
        place = place_ref[0]
        for step, w in enumerate((w0, w1, w2, w3)):
            wall[lax.rem(place + step, 4)] = w[...]

    start = pl.multiple_of(p * 128, 64)
    left = wall[lax.div(start, 192), pl.ds(pl.multiple_of(lax.rem(start, 192), 64), 64), :]
    start = start + 64
    right = wall[lax.div(start, 192), pl.ds(pl.multiple_of(lax.rem(start, 192), 64), 64), :]
    weights = jnp.concatenate([left, right], axis=0)
    values = jnp.concatenate([v0[0], v1[0], v2[0], v3[0]], axis=0)
    both = jnp.dot(weights, values, preferred_element_type=F32)
    first = first_head(I)
    for r in range(R):
        lanes = slice(r * 128, (r + 1) * 128)
        ctx[p, r * I : (r + 1) * I, :] = jnp.where(first, both[:I, lanes], both[I:, lanes]).astype(BF)

    @pl.when(p == PAIRS - 1)
    def _():
        context = jnp.concatenate([ctx[n] for n in range(PAIRS)], axis=1)
        update = jnp.dot(context, wo_ref[...], preferred_element_type=F32)
        after = (x_ref[...].astype(F32).reshape(R * I, D) + update).astype(BF)
        swap = reorder(R, I // 2)
        for half, ref in enumerate((first_ref, second_ref)):
            part = jnp.concatenate(
                [after[r * I + half * 32 : r * I + half * 32 + 32] for r in range(R)], axis=0
            )
            ref[...] = jnp.dot(swap, part, preferred_element_type=F32).astype(BF)


def row_context(place, weights, values, x, wo):
    whole = pl.BlockSpec((192, 512), lambda p: (0, 0))
    value = pl.BlockSpec((1, 128, R * 128), lambda p: (p, 0, 0))
    half = pl.BlockSpec((R * I // 2, D), lambda p: (0, 0))
    return pl.pallas_call(
        context_kernel,
        grid=(PAIRS,),
        out_shape=(jax.ShapeDtypeStruct((R * I // 2, D), BF),) * 2,
        in_specs=[pl.BlockSpec(memory_space=pltpu.SMEM)]
        + [whole] * 4
        + [value] * 4
        + [pl.BlockSpec((R, I, D), lambda p: (0, 0, 0)), pl.BlockSpec((D, D), lambda p: (0, 0))],
        out_specs=(half, half),
        scratch_shapes=[pltpu.VMEM((4, 192, 512), BF), pltpu.VMEM((PAIRS, R * I, 128), BF)],
        compiler_params=params(),
        cost_estimate=cost(2e9, 1e7),
        name="row_context",
    )(place, *weights, *values, x, wo)


def column_kernel(x_ref, w_ref, wo_ref, out_ref):
    x = x_ref[...].astype(F32).reshape(256, D)
    normed = layer_norm(x).astype(BF)
    qkv = jnp.dot(normed, w_ref[...], preferred_element_type=F32).astype(BF)
    first = first_head(256)
    zero = jnp.zeros((256, 128), BF)
    pieces = []
    for p in range(PAIRS):
        q = qkv[:, p * 128 : (p + 1) * 128]
        k = qkv[:, D + p * 128 : D + (p + 1) * 128]
        v = qkv[:, 2 * D + p * 128 : 2 * D + (p + 1) * 128]
        both = jnp.concatenate([jnp.where(first, q, zero), jnp.where(first, zero, q)], axis=0)
        scores = lax.dot_general(both, k, NT, preferred_element_type=F32)
        top = jnp.max(scores, axis=-1, keepdims=True)
        powers = jnp.exp2((scores - top) * (64**-0.5 * LOG2E))
        total = jnp.sum(powers, axis=-1, keepdims=True)
        mixed = jnp.dot(powers.astype(BF), v, preferred_element_type=F32) / total
        pieces.append(jnp.where(first, mixed[:256], mixed[256:]).astype(BF))
    context = jnp.concatenate(pieces, axis=1)
    update = jnp.dot(context, wo_ref[...], preferred_element_type=F32)
    out_ref[...] = (x + update).reshape(32, R, D).astype(BF)


def attend_column(x, w, wo):
    return pl.pallas_call(
        column_kernel,
        out_shape=jax.ShapeDtypeStruct((32, R, D), BF),
        in_specs=[VMEM] * 3,
        out_specs=VMEM,
        compiler_params=params(),
        cost_estimate=cost(2.5e9, 6e6, 800000),
        name="column",
    )(x, w, wo)


def finish_kernel(first_ref, second_ref, out_ref):
    swap = reorder(I // 2, R)
    for half, ref in enumerate((first_ref, second_ref)):
        rows = jnp.dot(swap, ref[...], preferred_element_type=F32).astype(BF)
        for r in range(R):
            out_ref[r, half * 32 : half * 32 + 32, :] = rows[r * 32 : r * 32 + 32]


def finish(first, second):
    return pl.pallas_call(
        finish_kernel,
        out_shape=jax.ShapeDtypeStruct((R, I, D), BF),
        in_specs=[VMEM] * 2,
        out_specs=VMEM,
        compiler_params=params(),
        cost_estimate=cost(4e8, 1.6e6),
        name="finish",
    )(first, second)


def shift(n, by):
    return [(i, (i + by) % n) for i in range(n)]


def per_device(x, w_row, wo_row, w_col, wo_col):
    seq = ("x", "z")
    other = functools.partial(lax.ppermute, axis_name="core", perm=shift(2, 1))
    partner = other(x)
    below = lax.ppermute(x, "y", shift(4, 1))
    above = lax.ppermute(x, "y", shift(4, 3))
    across = lax.ppermute(x, "y", shift(4, 2))
    q = masked_queries(x, w_row)
    parts = []
    values = []
    for own, mate in ((x, partner), (below, None), (above, None), (across, None)):
        mate = other(own) if mate is None else mate
        logits, v = keys_values(own, mate, w_row, q)
        values.append(v)
        logits = logits.reshape(32, 24, 128)
        parts.append(lax.all_to_all(logits, seq, 0, 0, tiled=True))
    scale = float((64 * 256) ** -0.5)
    copies = row_weights(parts, scale, 8)
    mine = lax.all_to_all(copies, "z", 0, 0, tiled=True).reshape(192, 512)
    weights = [mine] + [lax.ppermute(mine, "x", shift(4, -k)) for k in (1, 2, 3)]
    place = lax.axis_index("x").astype(jnp.int32).reshape(1)
    halves = row_context(place, weights, values, x, wo_row)
    done = []
    for half in halves:
        column = lax.all_to_all(half.reshape(32, R, D), seq, 0, 0, tiled=True)
        column = attend_column(column, w_col, wo_col)
        done.append(lax.all_to_all(column, seq, 0, 0, tiled=True).reshape(256, D))
    return finish(*done)


def solution(mesh):
    chips = Mesh(mesh.devices.reshape(4, 8, 4, 2), ("x", "z", "y", "core"))
    rows = P(("x", "z"), ("y", "core"), None)
    return jax.shard_map(
        per_device, mesh=chips, in_specs=(rows, P(), P(), P(), P()), out_specs=rows, check_vma=False
    )
```

```python
import functools

import jax
import jax.numpy as jnp
from jax import lax
from jax.experimental import pallas as pl
from jax.experimental.pallas import tpu as pltpu
from jax.sharding import Mesh, PartitionSpec as P

HEADS = 12
PAIRS = 6
D = 768
R = 8
I = 64
EPS = 1e-05
LOG2E = 1.4426950408889634
NT = (((1,), (1,)), ((), ()))
BF = jnp.bfloat16
F32 = jnp.float32
VMEM = pl.BlockSpec(memory_space=pltpu.VMEM)
MB = 1024 * 1024


def params(limit=48 * MB):
    return pltpu.CompilerParams(vmem_limit_bytes=limit)


def cost(flops, bytes_accessed, transcendentals=0):
    return pl.CostEstimate(
        flops=int(flops), bytes_accessed=int(bytes_accessed), transcendentals=int(transcendentals)
    )


def layer_norm(x):
    mean = jnp.mean(x, axis=-1, keepdims=True)
    centered = x - mean
    spread = jnp.mean(centered * centered, axis=-1, keepdims=True)
    return centered * lax.rsqrt(spread + EPS)


def first_head(rows):
    return lax.broadcasted_iota(jnp.int32, (rows, 128), 1) < 64


def store_block(ref, at, first, rows):
    for p in range(PAIRS):
        for r in range(rows.shape[0] // I):
            lanes = (first + r) * 128
            piece = rows[r * I : (r + 1) * I, p * 128 : (p + 1) * 128]
            ref[p, at : at + I, lanes : lanes + 128] = piece


def store_logits(place_ref, q_ref, keys, rows, out_refs):
    first = lax.rem(lax.broadcasted_iota(jnp.int32, (I, R * 128), 1), 128) < 64
    zero = jnp.zeros((I, R * 128), BF)
    core, place = place_ref[0], place_ref[1]
    for p in range(PAIRS):
        masked = []
        for part in range(2):
            q = q_ref[p, part * I : (part + 1) * I]
            masked += [jnp.where(first, q, zero), jnp.where(first, zero, q)]
        logits = lax.dot_general(
            jnp.concatenate(masked, axis=0), keys[p], NT, preferred_element_type=F32
        )
        for n in range(4):
            group, at = divmod(2 * p + n % 2, 3)
            owner = core if n < 2 else 1 - core
            rows[owner, group, at * I : (at + 1) * I] = logits[n * I : (n + 1) * I]
    for k, ref in enumerate(out_refs):
        group = lax.rem(place + k, 4)
        both = [rows[c, group].reshape(8, 24, 128) for c in range(2)]
        ref[...] = jnp.concatenate(both, axis=1).astype(BF)


def normed_rows(ref, s):
    return layer_norm(ref[4 * s : 4 * s + 4].astype(F32).reshape(4 * I, D)).astype(BF)


def project(rows, w_ref):
    return jnp.dot(rows, w_ref[...], preferred_element_type=F32).astype(BF)


def own_kernel(x_ref, mate_ref, wq_ref, wk_ref, wv_ref, q_ref, k_ref, v_ref):
    for s in range(2):
        rows = normed_rows(x_ref, s)
        store_block(q_ref, 0, 4 * s, project(rows, wq_ref))
        store_block(k_ref, 0, 4 * s, project(rows, wk_ref))
        store_block(v_ref, 0, 4 * s, project(rows, wv_ref))
        store_block(q_ref, I, 4 * s, project(normed_rows(mate_ref, s), wq_ref))


def near_kernel(place_ref, key_ref, a_ref, b_ref, wk_ref, q_ref, wv_ref, *refs):
    out_refs, (v_ref, bkey_ref, keys, rows) = refs[:4], refs[4:]
    keys[:, :I] = key_ref[...]
    for s in range(2):
        normed = normed_rows(a_ref, s)
        store_block(keys, I, 4 * s, project(normed, wk_ref))
        store_block(v_ref, 0, 4 * s, project(normed, wv_ref))
    store_logits(place_ref, q_ref, keys, rows, out_refs)
    for s in range(2):
        normed = normed_rows(b_ref, s)
        store_block(bkey_ref, 0, 4 * s, project(normed, wk_ref))
        store_block(v_ref, I, 4 * s, project(normed, wv_ref))


def far_kernel(place_ref, key_ref, far_ref, wk_ref, q_ref, *refs):
    out_refs, (keys, rows) = refs[:4], refs[4:]
    keys[:, :I] = key_ref[...]
    for s in range(2):
        store_block(keys, I, 4 * s, project(normed_rows(far_ref, s), wk_ref))
    store_logits(place_ref, q_ref, keys, rows, out_refs)


def value_kernel(far_ref, wv_ref, v_ref):
    for s in range(2):
        store_block(v_ref, 0, 4 * s, project(normed_rows(far_ref, s), wv_ref))


SMEM = pl.BlockSpec(memory_space=pltpu.SMEM)


def block(*shape):
    return pl.BlockSpec(shape, lambda s: (0,) * len(shape))


def weight(part):
    return pl.BlockSpec((D, D), lambda s: (0, part))


LOGITS = jax.ShapeDtypeStruct((8, 48, 128), BF)
ONE = jax.ShapeDtypeStruct((PAIRS, I, R * 128), BF)
TWO = jax.ShapeDtypeStruct((PAIRS, 2 * I, R * 128), BF)
ROWS = pltpu.VMEM((2, 4, 192, 128), F32)
KEYS = pltpu.VMEM((PAIRS, 128, R * 128), BF)


def own_projections(x, mate, w):
    whole, one, two = block(R, I, D), block(*ONE.shape), block(*TWO.shape)
    return pl.pallas_call(
        own_kernel,
        grid=(1,),
        out_shape=(TWO, ONE, ONE),
        in_specs=[whole, whole, weight(0), weight(1), weight(2)],
        out_specs=(two, one, one),
        compiler_params=params(64 * MB),
        cost_estimate=cost(2.4e9, 9e6),
        name="own_projections",
    )(x, mate, w, w, w)


def near_logits(place, keys, a, b, w, q):
    whole, one, two = block(R, I, D), block(*ONE.shape), block(*TWO.shape)
    return pl.pallas_call(
        near_kernel,
        grid=(1,),
        out_shape=[LOGITS] * 4 + [TWO, ONE],
        in_specs=[SMEM, one, whole, whole, weight(1), two, weight(2)],
        out_specs=[block(8, 48, 128)] * 4 + [two, one],
        scratch_shapes=[KEYS, ROWS],
        compiler_params=params(64 * MB),
        cost_estimate=cost(4e9, 9e6),
        name="near_logits",
    )(place, keys, a, b, w, q, w)


def far_logits(place, keys, far, w, q):
    return pl.pallas_call(
        far_kernel,
        grid=(1,),
        out_shape=[LOGITS] * 4,
        in_specs=[SMEM, block(*ONE.shape), block(R, I, D), weight(1), block(*TWO.shape)],
        out_specs=[block(8, 48, 128)] * 4,
        scratch_shapes=[KEYS, ROWS],
        compiler_params=params(64 * MB),
        cost_estimate=cost(2e9, 6e6),
        name="far_logits",
    )(place, keys, far, w, q)


def far_values(far, w):
    return pl.pallas_call(
        value_kernel,
        grid=(1,),
        out_shape=ONE,
        in_specs=[block(R, I, D), weight(2)],
        out_specs=block(*ONE.shape),
        compiler_params=params(64 * MB),
        cost_estimate=cost(1.2e9, 4e6),
        name="far_values",
    )(far, w)


def gather_kernel(*refs):
    out_ref = refs[-1]
    for half in range(2):
        total = refs[4 * half][...].astype(F32)
        for ref in refs[4 * half + 1 : 4 * half + 4]:
            total += ref[...].astype(F32)
        out_ref[:, :, half * 128 : half * 128 + 128] = total.astype(BF)


def sum_x(near, far):
    return pl.pallas_call(
        gather_kernel,
        out_shape=jax.ShapeDtypeStruct((8, 48, 256), BF),
        in_specs=[VMEM] * 8,
        out_specs=VMEM,
        compiler_params=params(64 * MB),
        cost_estimate=cost(1e6, 1e6),
        name="sum_x",
    )(*near, *far)


def sum_kernel(place_ref, parts_ref, mine_ref, mates_ref, rows):
    rows[...] = jnp.sum(parts_ref[...].astype(F32), axis=0).reshape(2, 24, 256)
    core = place_ref[0]
    mine_ref[...] = rows[core]
    mates_ref[...] = rows[1 - core]


def sum_z(place, parts):
    return pl.pallas_call(
        sum_kernel,
        out_shape=(jax.ShapeDtypeStruct((24, 256), F32),) * 2,
        in_specs=[SMEM, VMEM],
        out_specs=(VMEM, VMEM),
        scratch_shapes=[pltpu.VMEM((2, 24, 256), F32)],
        compiler_params=params(),
        cost_estimate=cost(1e6, 1e6),
        name="sum_z",
    )(place, parts)


def weight_kernel(scale, copies, near_ref, far_ref, out_ref):
    logits = jnp.concatenate([near_ref[...], far_ref[...]], axis=1)
    top = jnp.max(logits, axis=-1, keepdims=True)
    powers = jnp.exp2((logits - top) * (scale * LOG2E))
    weights = (powers / jnp.sum(powers, axis=-1, keepdims=True)).astype(BF)
    for c in range(copies):
        out_ref[c] = weights


def row_weights(own, mates, scale, copies):
    return pl.pallas_call(
        functools.partial(weight_kernel, scale, copies),
        out_shape=jax.ShapeDtypeStruct((copies, 24, 512), BF),
        in_specs=[VMEM] * 2,
        out_specs=VMEM,
        compiler_params=params(),
        cost_estimate=cost(1e6, 1e6),
        name="row_weights",
    )(own, mates)


def reorder(major, minor):
    n = major * minor
    to = lax.broadcasted_iota(jnp.int32, (n, n), 0)
    at = lax.broadcasted_iota(jnp.int32, (n, n), 1)
    source = lax.rem(to, major) * minor + lax.div(to, major)
    return jnp.where(at == source, 1.0, 0.0).astype(BF)


def context_kernel(place_ref, w0, w1, w2, w3, *refs):
    value_refs, (x_ref, wo_ref, out_ref, wall, ctx) = refs[:6], refs[6:]
    p = pl.program_id(0)

    @pl.when(p == 0)
    def _():
        place = place_ref[1]
        for step, w in enumerate((w0, w1, w2, w3)):
            wall[lax.rem(place + step, 4)] = w[...]

    start = pl.multiple_of(p * 128, 64)
    left = wall[lax.div(start, 192), pl.ds(pl.multiple_of(lax.rem(start, 192), 64), 64), :]
    start = start + 64
    right = wall[lax.div(start, 192), pl.ds(pl.multiple_of(lax.rem(start, 192), 64), 64), :]
    weights = jnp.concatenate([left, right], axis=0)
    values = jnp.concatenate([ref[0] for ref in value_refs], axis=0)
    both = jnp.dot(weights, values, preferred_element_type=F32)
    first = first_head(I)
    for r in range(R):
        lanes = slice(r * 128, (r + 1) * 128)
        ctx[p, r * I : (r + 1) * I, :] = jnp.where(first, both[:I, lanes], both[I:, lanes]).astype(BF)

    @pl.when(p == PAIRS - 1)
    def _():
        context = jnp.concatenate([ctx[n] for n in range(PAIRS)], axis=1)
        update = jnp.dot(context, wo_ref[...], preferred_element_type=F32)
        after = (x_ref[...].astype(F32).reshape(R * I, D) + update).astype(BF)
        out_ref[...] = jnp.dot(reorder(R, I), after, preferred_element_type=F32).astype(BF)


def row_context(place, weights, values, x, wo):
    whole = pl.BlockSpec((192, 512), lambda p: (0, 0))
    value = [pl.BlockSpec((1, v.shape[1], R * 128), lambda p: (p, 0, 0)) for v in values]
    return pl.pallas_call(
        context_kernel,
        grid=(PAIRS,),
        out_shape=jax.ShapeDtypeStruct((R * I, D), BF),
        in_specs=[pl.BlockSpec(memory_space=pltpu.SMEM)]
        + [whole] * 4
        + value
        + [pl.BlockSpec((R, I, D), lambda p: (0, 0, 0)), pl.BlockSpec((D, D), lambda p: (0, 0))],
        out_specs=pl.BlockSpec((R * I, D), lambda p: (0, 0)),
        scratch_shapes=[pltpu.VMEM((4, 192, 512), BF), pltpu.VMEM((PAIRS, R * I, 128), BF)],
        compiler_params=params(64 * MB),
        cost_estimate=cost(2e9, 1e7),
        name="row_context",
    )(place, *weights, *values, x, wo)


def column_kernel(x_ref, wq_ref, wk_ref, wv_ref, wo_ref, out_ref, normed, total):
    g = pl.program_id(0)

    def column(c):
        return x_ref[...].astype(F32).reshape(32, 2, R, D)[:, c].reshape(256, D)

    @pl.when(g == 0)
    def _():
        for c in range(2):
            normed[c * 256 : (c + 1) * 256] = layer_norm(column(c)).astype(BF)

    rows = normed[...]
    q = jnp.dot(rows, wq_ref[...], preferred_element_type=F32).astype(BF)
    k = jnp.dot(rows, wk_ref[...], preferred_element_type=F32).astype(BF)
    v = jnp.dot(rows, wv_ref[...], preferred_element_type=F32).astype(BF)
    first = first_head(256)
    zero = jnp.zeros((256, 128), BF)
    contexts = []
    for c in range(2):
        pieces = []
        for p in range(2):
            at = (slice(c * 256, (c + 1) * 256), slice(p * 128, (p + 1) * 128))
            both = jnp.concatenate(
                [jnp.where(first, q[at], zero), jnp.where(first, zero, q[at])], axis=0
            )
            scores = lax.dot_general(both, k[at], NT, preferred_element_type=F32)
            top = jnp.max(scores, axis=-1, keepdims=True)
            powers = jnp.exp2((scores - top) * (64**-0.5 * LOG2E))
            weight = jnp.sum(powers, axis=-1, keepdims=True)
            mixed = jnp.dot(powers.astype(BF), v[at], preferred_element_type=F32) / weight
            pieces.append(jnp.where(first, mixed[:256], mixed[256:]).astype(BF))
        contexts.append(jnp.concatenate(pieces, axis=1))
    context = jnp.concatenate(contexts, axis=0)
    update = jnp.dot(context, wo_ref[...], preferred_element_type=F32)

    @pl.when(g == 0)
    def _():
        total[...] = update

    @pl.when(g == 1)
    def _():
        total[...] += update

    @pl.when(g == 2)
    def _():
        done = total[...] + update
        both = [(column(c) + done[c * 256 : (c + 1) * 256]).reshape(32, R, D) for c in range(2)]
        out_ref[...] = jnp.concatenate(both, axis=1).astype(BF)


def attend_columns(x, w, wo):
    whole = pl.BlockSpec((32, 2 * R, D), lambda g: (0, 0, 0))
    return pl.pallas_call(
        column_kernel,
        grid=(3,),
        out_shape=jax.ShapeDtypeStruct((32, 2 * R, D), BF),
        in_specs=[
            whole,
            pl.BlockSpec((D, 256), lambda g: (0, g)),
            pl.BlockSpec((D, 256), lambda g: (0, g + 3)),
            pl.BlockSpec((D, 256), lambda g: (0, g + 6)),
            pl.BlockSpec((256, D), lambda g: (g, 0)),
        ],
        out_specs=whole,
        scratch_shapes=[pltpu.VMEM((512, D), BF), pltpu.VMEM((512, D), F32)],
        compiler_params=params(),
        cost_estimate=cost(5e9, 7e6, 1600000),
        name="columns",
    )(x, w, w, w, wo)


def finish_kernel(x_ref, out_ref):
    rows = jnp.dot(reorder(I, R), x_ref[...], preferred_element_type=F32).astype(BF)
    for r in range(R):
        out_ref[r] = rows[r * I : (r + 1) * I]


def finish(x):
    return pl.pallas_call(
        finish_kernel,
        out_shape=jax.ShapeDtypeStruct((R, I, D), BF),
        in_specs=[VMEM],
        out_specs=VMEM,
        compiler_params=params(),
        cost_estimate=cost(4e8, 1.6e6),
        name="finish",
    )(x)


def shift(n, by):
    return [(i, (i + by) % n) for i in range(n)]


def per_device(x, w_row, wo_row, w_col, wo_col):
    seq = ("x", "z")
    mate = functools.partial(lax.ppermute, axis_name="core", perm=shift(2, 1))
    ways = [[(2 * y + c, 2 * ((y + 1 - 2 * c) % 4) + c) for y in range(4) for c in range(2)]]
    ways.append([(b, a) for a, b in ways[0]])
    on, back = [functools.partial(lax.ppermute, axis_name=("y", "core"), perm=way) for way in ways]
    along = [functools.partial(lax.ppermute, axis_name="x", perm=shift(4, k)) for k in range(4)]
    place = jnp.stack([lax.axis_index("core"), lax.axis_index("x")]).astype(jnp.int32)

    a, b = on(x), back(x)
    q, keys, own_values = own_projections(x, mate(x), w_row)
    a, b, q = lax.optimization_barrier((a, b, q))
    far = on(a)
    *near, near_values, keys = near_logits(place, keys, a, b, w_row, q)
    near = [near[0]] + [along[k](near[k]) for k in (1, 2, 3)]
    far, keys = lax.optimization_barrier((far, keys))
    partial = far_logits(place, keys, far, w_row, q)
    ordered = lax.optimization_barrier((*near, *partial))
    near, partial = ordered[:4], ordered[4:]
    partial = [partial[0]] + [along[k](partial[k]) for k in (1, 2, 3)]
    far, sums = lax.optimization_barrier((far, sum_x(near, partial)))
    parts = lax.all_to_all(sums, "z", 0, 0, tiled=True)
    values = far_values(far, w_row)
    parts, values = lax.optimization_barrier((parts, values))
    values = [own_values, near_values, values]
    values += [mate(v) for v in values]
    own, other = sum_z(place, parts)
    copies = row_weights(own, mate(other), float((64 * 256) ** -0.5), 8)
    mine = lax.all_to_all(copies, "z", 0, 0, tiled=True).reshape(192, 512)
    weights = [mine] + [along[4 - k](mine) for k in (1, 2, 3)]
    rows = row_context(place, weights, values, x, wo_row)
    columns = lax.all_to_all(rows.reshape(32, 2 * R, D), seq, 0, 0, tiled=True)
    columns = attend_columns(columns, w_col, wo_col)
    rows = lax.all_to_all(columns, seq, 0, 0, tiled=True)
    return finish(rows.reshape(R * I, D))


def solution(mesh):
    chips = Mesh(mesh.devices.reshape(4, 8, 4, 2), ("x", "z", "y", "core"))
    rows = P(("x", "z"), ("y", "core"), None)
    return jax.shard_map(
        per_device, mesh=chips, in_specs=(rows, P(), P(), P(), P()), out_specs=rows, check_vma=False
    )
```

```python
import functools

import jax
import jax.numpy as jnp
from jax import lax
from jax.experimental import pallas as pl
from jax.experimental.pallas import tpu as pltpu
from jax.sharding import Mesh, PartitionSpec as P

HEADS = 12
PAIRS = 6
D = 768
R = 8
I = 64
EPS = 1e-05
LOG2E = 1.4426950408889634
NT = (((1,), (1,)), ((), ()))
BF = jnp.bfloat16
F32 = jnp.float32
VMEM = pl.BlockSpec(memory_space=pltpu.VMEM)
MB = 1024 * 1024


def params(limit=48 * MB):
    return pltpu.CompilerParams(vmem_limit_bytes=limit)


def cost(flops, bytes_accessed, transcendentals=0):
    return pl.CostEstimate(
        flops=int(flops), bytes_accessed=int(bytes_accessed), transcendentals=int(transcendentals)
    )


def layer_norm(x):
    mean = jnp.mean(x, axis=-1, keepdims=True)
    centered = x - mean
    spread = jnp.mean(centered * centered, axis=-1, keepdims=True)
    return centered * lax.rsqrt(spread + EPS)


def first_head(rows):
    return lax.broadcasted_iota(jnp.int32, (rows, 128), 1) < 64


def store_block(ref, at, first, rows):
    for p in range(PAIRS):
        for r in range(rows.shape[0] // I):
            lanes = (first + r) * 128
            piece = rows[r * I : (r + 1) * I, p * 128 : (p + 1) * 128]
            ref[p, at : at + I, lanes : lanes + 128] = piece


def store_logits(q_ref, keys, rows, out_ref):
    first = lax.rem(lax.broadcasted_iota(jnp.int32, (I, R * 128), 1), 128) < 64
    zero = jnp.zeros((I, R * 128), BF)
    core = lax.axis_index("core")
    for p in range(PAIRS):
        masked = []
        for part in range(2):
            q = q_ref[p, part * I : (part + 1) * I]
            masked += [jnp.where(first, q, zero), jnp.where(first, zero, q)]
        logits = lax.dot_general(
            jnp.concatenate(masked, axis=0), keys[p], NT, preferred_element_type=F32
        )
        rows[core, p * 128 : (p + 1) * 128] = logits[:128]
        rows[1 - core, p * 128 : (p + 1) * 128] = logits[128:]
    both = [rows[c].reshape(32, 24, 128) for c in range(2)]
    out_ref[...] = jnp.concatenate(both, axis=1).astype(BF)


def normed_rows(ref, s):
    return layer_norm(ref[4 * s : 4 * s + 4].astype(F32).reshape(4 * I, D)).astype(BF)


def project(rows, w_ref):
    return jnp.dot(rows, w_ref[...], preferred_element_type=F32).astype(BF)


def own_kernel(x_ref, mate_ref, wq_ref, wk_ref, wv_ref, q_ref, k_ref, v_ref):
    for s in range(2):
        rows = normed_rows(x_ref, s)
        store_block(q_ref, 0, 4 * s, project(rows, wq_ref))
        store_block(k_ref, 0, 4 * s, project(rows, wk_ref))
        store_block(v_ref, 0, 4 * s, project(rows, wv_ref))
        store_block(q_ref, I, 4 * s, project(normed_rows(mate_ref, s), wq_ref))


def near_kernel(key_ref, a_ref, wk_ref, q_ref, out_ref, keys, rows):
    keys[:, :I] = key_ref[...]
    for s in range(2):
        store_block(keys, I, 4 * s, project(normed_rows(a_ref, s), wk_ref))
    store_logits(q_ref, keys, rows, out_ref)


def far_kernel(b_ref, far_ref, wk_ref, q_ref, out_ref, keys, rows):
    for at, ref in ((0, b_ref), (I, far_ref)):
        for s in range(2):
            store_block(keys, at, 4 * s, project(normed_rows(ref, s), wk_ref))
    store_logits(q_ref, keys, rows, out_ref)


def value_kernel(a_ref, b_ref, far_ref, wv_ref, v_ref):
    for n, ref in enumerate((a_ref, b_ref, far_ref)):
        for s in range(2):
            store_block(v_ref, n * I, 4 * s, project(normed_rows(ref, s), wv_ref))


def block(*shape):
    return pl.BlockSpec(shape, lambda s: (0,) * len(shape))


def weight(part):
    return pl.BlockSpec((D, D), lambda s: (0, part))


LOGITS = jax.ShapeDtypeStruct((32, 48, 128), BF)
ONE = jax.ShapeDtypeStruct((PAIRS, I, R * 128), BF)
TWO = jax.ShapeDtypeStruct((PAIRS, 2 * I, R * 128), BF)
ROWS = pltpu.VMEM((2, D, 128), F32)
KEYS = pltpu.VMEM((PAIRS, 128, R * 128), BF)


def own_projections(x, mate, w):
    whole, one, two = block(R, I, D), block(*ONE.shape), block(*TWO.shape)
    return pl.pallas_call(
        own_kernel,
        grid=(1,),
        out_shape=(TWO, ONE, ONE),
        in_specs=[whole, whole, weight(0), weight(1), weight(2)],
        out_specs=(two, one, one),
        compiler_params=params(64 * MB),
        cost_estimate=cost(2.4e9, 9e6),
        name="own_projections",
    )(x, mate, w, w, w)


def near_logits(keys, a, w, q):
    whole, one, two = block(R, I, D), block(*ONE.shape), block(*TWO.shape)
    return pl.pallas_call(
        near_kernel,
        grid=(1,),
        out_shape=LOGITS,
        in_specs=[one, whole, weight(1), two],
        out_specs=block(32, 48, 128),
        scratch_shapes=[KEYS, ROWS],
        compiler_params=params(64 * MB),
        cost_estimate=cost(3e9, 8e6),
        name="near_logits",
    )(keys, a, w, q)


def far_logits(b, far, w, q):
    whole = block(R, I, D)
    return pl.pallas_call(
        far_kernel,
        grid=(1,),
        out_shape=LOGITS,
        in_specs=[whole, whole, weight(1), block(*TWO.shape)],
        out_specs=block(32, 48, 128),
        scratch_shapes=[KEYS, ROWS],
        compiler_params=params(64 * MB),
        cost_estimate=cost(3e9, 7e6),
        name="far_logits",
    )(b, far, w, q)


def other_values(a, b, far, w):
    whole, three = block(R, I, D), (PAIRS, 3 * I, R * 128)
    return pl.pallas_call(
        value_kernel,
        grid=(1,),
        out_shape=jax.ShapeDtypeStruct(three, BF),
        in_specs=[whole, whole, whole, weight(2)],
        out_specs=block(*three),
        compiler_params=params(64 * MB),
        cost_estimate=cost(2e9, 6e6),
        name="other_values",
    )(a, b, far, w)


def sum_kernel(near_ref, far_ref, mine_ref, mates_ref, rows):
    totals = [jnp.sum(ref[...].astype(F32), axis=0) for ref in (near_ref, far_ref)]
    rows[...] = jnp.concatenate(totals, axis=1).reshape(2, 24, 256)
    core = lax.axis_index("core")
    mine_ref[...] = rows[core]
    mates_ref[...] = rows[1 - core]


def sum_logits(near, far):
    return pl.pallas_call(
        sum_kernel,
        out_shape=(jax.ShapeDtypeStruct((24, 256), F32),) * 2,
        in_specs=[VMEM, VMEM],
        out_specs=(VMEM, VMEM),
        scratch_shapes=[pltpu.VMEM((2, 24, 256), F32)],
        compiler_params=params(),
        cost_estimate=cost(1e6, 1e6),
        name="sum_logits",
    )(near, far)


def weight_kernel(scale, copies, near_ref, far_ref, out_ref):
    logits = jnp.concatenate([near_ref[...], far_ref[...]], axis=1)
    top = jnp.max(logits, axis=-1, keepdims=True)
    powers = jnp.exp2((logits - top) * (scale * LOG2E))
    weights = (powers / jnp.sum(powers, axis=-1, keepdims=True)).astype(BF)
    for c in range(copies):
        out_ref[c] = weights


def row_weights(own, mates, scale, copies):
    return pl.pallas_call(
        functools.partial(weight_kernel, scale, copies),
        out_shape=jax.ShapeDtypeStruct((copies, 24, 512), BF),
        in_specs=[VMEM] * 2,
        out_specs=VMEM,
        compiler_params=params(),
        cost_estimate=cost(1e6, 1e6),
        name="row_weights",
    )(own, mates)


def reorder(major, minor):
    n = major * minor
    to = lax.broadcasted_iota(jnp.int32, (n, n), 0)
    at = lax.broadcasted_iota(jnp.int32, (n, n), 1)
    source = lax.rem(to, major) * minor + lax.div(to, major)
    return jnp.where(at == source, 1.0, 0.0).astype(BF)


HBM = pl.BlockSpec(memory_space=pltpu.HBM)


STEP = 3


def context_kernel(w0, w1, w2, w3, *refs):
    value_refs, (x_ref, wo_ref, out_ref), refs = refs[:4], refs[4:7], refs[7:]
    wall, ctx, x_own, wo, sems = refs
    g = pl.program_id(0)
    late = [
        pltpu.make_async_copy(wo_ref, wo, sems.at[0]),
        pltpu.make_async_copy(x_ref, x_own, sems.at[1]),
    ]

    @pl.when(g == 0)
    def _():
        place = lax.axis_index("x")
        for step, w in enumerate((w0, w1, w2, w3)):
            wall[lax.rem(place + step, 4)] = w[...].reshape(3, I, 512)
        for copy in late:
            copy.start()

    first = first_head(I)
    for n in range(STEP):
        pair = []
        for h in range(2):
            head = (g * STEP + n) * 2 + h
            pair.append(wall[lax.div(head, 3), lax.rem(head, 3)])
        weights = jnp.concatenate(pair, axis=0)
        values = jnp.concatenate([ref[n] for ref in value_refs], axis=0)
        both = jnp.dot(weights, values, preferred_element_type=F32)
        for r in range(R):
            lanes = slice(r * 128, (r + 1) * 128)
            piece = jnp.where(first, both[:I, lanes], both[I:, lanes]).astype(BF)
            ctx[g * STEP + n, r * I : (r + 1) * I, :] = piece

    @pl.when(g == PAIRS // STEP - 1)
    def _():
        for copy in late:
            copy.wait()
        context = jnp.concatenate([ctx[n] for n in range(PAIRS)], axis=1)
        update = jnp.dot(context, wo[...], preferred_element_type=F32)
        after = (x_own[...].astype(F32).reshape(R * I, D) + update).astype(BF)
        out_ref[...] = jnp.dot(reorder(R, I), after, preferred_element_type=F32).astype(BF)


def row_context(weights, values, x, wo):
    whole = pl.BlockSpec((192, 512), lambda p: (0, 0))
    value = [pl.BlockSpec((STEP, v.shape[1], R * 128), lambda p: (p, 0, 0)) for v in values]
    return pl.pallas_call(
        context_kernel,
        grid=(PAIRS // STEP,),
        out_shape=jax.ShapeDtypeStruct((R * I, D), BF),
        in_specs=[whole] * 4
        + value
        + [HBM, HBM],
        out_specs=pl.BlockSpec((R * I, D), lambda p: (0, 0)),
        scratch_shapes=[
            pltpu.VMEM((4, 3, I, 512), BF),
            pltpu.VMEM((PAIRS, R * I, 128), BF),
            pltpu.VMEM((R, I, D), BF),
            pltpu.VMEM((D, D), BF),
            pltpu.SemaphoreType.DMA((2,)),
        ],
        compiler_params=params(62 * MB),
        cost_estimate=cost(2e9, 1e7),
        name="row_context",
    )(*weights, *values, x, wo)


def column_kernel(x_ref, wq_ref, wk_ref, wv_ref, wo_ref, out_ref, normed, context, wo, sem):
    g = pl.program_id(0)
    late = pltpu.make_async_copy(wo_ref, wo, sem)

    def column(c):
        return x_ref[...].astype(F32).reshape(32, 2, R, D)[:, c].reshape(256, D)

    @pl.when(g == 0)
    def _():
        late.start()
        for c in range(2):
            normed[c * 256 : (c + 1) * 256] = layer_norm(column(c)).astype(BF)

    rows = normed[...]
    q = jnp.dot(rows, wq_ref[...], preferred_element_type=F32).astype(BF)
    k = jnp.dot(rows, wk_ref[...], preferred_element_type=F32).astype(BF)
    v = jnp.dot(rows, wv_ref[...], preferred_element_type=F32).astype(BF)
    first = first_head(256)
    zero = jnp.zeros((256, 128), BF)
    for c in range(2):
        rows = slice(c * 256, (c + 1) * 256)
        for p in range(2):
            at = (rows, slice(p * 128, (p + 1) * 128))
            both = jnp.concatenate(
                [jnp.where(first, q[at], zero), jnp.where(first, zero, q[at])], axis=0
            )
            scores = lax.dot_general(both, k[at], NT, preferred_element_type=F32)
            top = jnp.max(scores, axis=-1, keepdims=True)
            powers = jnp.exp2((scores - top) * (64**-0.5 * LOG2E))
            weight = jnp.sum(powers, axis=-1, keepdims=True)
            mixed = jnp.dot(powers.astype(BF), v[at], preferred_element_type=F32) / weight
            context[2 * g + p, rows] = jnp.where(first, mixed[:256], mixed[256:]).astype(BF)

    @pl.when(g == 2)
    def _():
        late.wait()
        whole = jnp.concatenate([context[p] for p in range(PAIRS)], axis=1)
        update = jnp.dot(whole, wo[...], preferred_element_type=F32)
        both = [(column(c) + update[c * 256 : (c + 1) * 256]).reshape(32, R, D) for c in range(2)]
        out_ref[...] = jnp.concatenate(both, axis=1).astype(BF)


def attend_columns(x, w, wo):
    whole = pl.BlockSpec((32, 2 * R, D), lambda g: (0, 0, 0))
    return pl.pallas_call(
        column_kernel,
        grid=(3,),
        out_shape=jax.ShapeDtypeStruct((32, 2 * R, D), BF),
        in_specs=[
            whole,
            pl.BlockSpec((D, 256), lambda g: (0, g)),
            pl.BlockSpec((D, 256), lambda g: (0, g + 3)),
            pl.BlockSpec((D, 256), lambda g: (0, g + 6)),
            HBM,
        ],
        out_specs=whole,
        scratch_shapes=[
            pltpu.VMEM((512, D), BF),
            pltpu.VMEM((PAIRS, 512, 128), BF),
            pltpu.VMEM((D, D), BF),
            pltpu.SemaphoreType.DMA,
        ],
        compiler_params=params(62 * MB),
        cost_estimate=cost(5e9, 7e6, 1600000),
        name="columns",
    )(x, w, w, w, wo)


def finish_kernel(x_ref, out_ref):
    rows = jnp.dot(reorder(I, R), x_ref[...], preferred_element_type=F32).astype(BF)
    for r in range(R):
        out_ref[r] = rows[r * I : (r + 1) * I]


def finish(x):
    return pl.pallas_call(
        finish_kernel,
        out_shape=jax.ShapeDtypeStruct((R, I, D), BF),
        in_specs=[VMEM],
        out_specs=VMEM,
        compiler_params=params(),
        cost_estimate=cost(4e8, 1.6e6),
        name="finish",
    )(x)


def shift(n, by):
    return [(i, (i + by) % n) for i in range(n)]


def per_device(x, w_row, wo_row, w_col, wo_col):
    exchange = functools.partial(
        lax.all_to_all, axis_name=("x", "z"), split_axis=0, concat_axis=0, tiled=True
    )
    mate = functools.partial(lax.ppermute, axis_name="core", perm=shift(2, 1))
    ways = [[(2 * y + c, 2 * ((y + 1 - 2 * c) % 4) + c) for y in range(4) for c in range(2)]]
    ways.append([(b, a) for a, b in ways[0]])
    on, back = [functools.partial(lax.ppermute, axis_name=("y", "core"), perm=way) for way in ways]
    along = [functools.partial(lax.ppermute, axis_name="x", perm=shift(4, k)) for k in range(4)]

    a = on(x)
    q, keys, own_values = own_projections(x, mate(x), w_row)
    later, q = lax.optimization_barrier((x, q))
    b, far = back(later), on(a)
    near = near_logits(keys, a, w_row, q)
    b, far, _ = lax.optimization_barrier((b, far, near))
    near = exchange(near)
    logits = far_logits(b, far, w_row, q)
    a, b, far, logits, near = lax.optimization_barrier((a, b, far, logits, near))
    logits = exchange(logits)
    values = other_values(a, b, far, w_row)
    logits, values = lax.optimization_barrier((logits, values))
    values = [own_values, values]
    values += [mate(v) for v in values]
    own, other = sum_logits(near, logits)
    copies = row_weights(own, mate(other), float((64 * 256) ** -0.5), 8)
    mine = lax.all_to_all(copies, "z", 0, 0, tiled=True).reshape(192, 512)
    weights = [mine] + [along[4 - k](mine) for k in (1, 2, 3)]
    rows = row_context(weights, values, x, wo_row)
    columns = exchange(rows.reshape(32, 2 * R, D))
    columns = attend_columns(columns, w_col, wo_col)
    rows = exchange(columns)
    return finish(rows.reshape(R * I, D))


def solution(mesh):
    chips = Mesh(mesh.devices.reshape(4, 8, 4, 2), ("x", "z", "y", "core"))
    rows = P(("x", "z"), ("y", "core"), None)
    return jax.shard_map(
        per_device, mesh=chips, in_specs=(rows, P(), P(), P(), P()), out_specs=rows, check_vma=False
    )
```

```python
import functools

import jax
import jax.numpy as jnp
from jax import lax
from jax.experimental import pallas as pl
from jax.experimental.pallas import tpu as pltpu
from jax.sharding import Mesh, PartitionSpec as P

HEADS = 12
PAIRS = 6
D = 768
R = 8
I = 64
EPS = 1e-05
LOG2E = 1.4426950408889634
NT = (((1,), (1,)), ((), ()))
BF = jnp.bfloat16
F32 = jnp.float32
VMEM = pl.BlockSpec(memory_space=pltpu.VMEM)
MB = 1024 * 1024


def params(limit=48 * MB):
    return pltpu.CompilerParams(vmem_limit_bytes=limit)


def cost(flops, bytes_accessed, transcendentals=0):
    return pl.CostEstimate(
        flops=int(flops), bytes_accessed=int(bytes_accessed), transcendentals=int(transcendentals)
    )


def layer_norm(x):
    mean = jnp.mean(x, axis=-1, keepdims=True)
    centered = x - mean
    spread = jnp.mean(centered * centered, axis=-1, keepdims=True)
    return centered * lax.rsqrt(spread + EPS)


def first_head(rows):
    return lax.broadcasted_iota(jnp.int32, (rows, 128), 1) < 64


def store_block(ref, at, first, rows):
    for p in range(PAIRS):
        for r in range(rows.shape[0] // I):
            lanes = (first + r) * 128
            piece = rows[r * I : (r + 1) * I, p * 128 : (p + 1) * 128]
            ref[p, at : at + I, lanes : lanes + 128] = piece


def store_logits(q_ref, keys, rows, out_ref):
    first = lax.rem(lax.broadcasted_iota(jnp.int32, (I, R * 128), 1), 128) < 64
    zero = jnp.zeros((I, R * 128), BF)
    core = lax.axis_index("core")
    for p in range(PAIRS):
        masked = []
        for part in range(2):
            q = q_ref[p, part * I : (part + 1) * I]
            masked += [jnp.where(first, q, zero), jnp.where(first, zero, q)]
        logits = lax.dot_general(
            jnp.concatenate(masked, axis=0), keys[p], NT, preferred_element_type=F32
        )
        rows[core, p * 128 : (p + 1) * 128] = logits[:128]
        rows[1 - core, p * 128 : (p + 1) * 128] = logits[128:]
    both = [rows[c].reshape(32, 24, 128) for c in range(2)]
    out_ref[...] = jnp.concatenate(both, axis=1).astype(BF)


def normed_rows(ref, s):
    return layer_norm(ref[4 * s : 4 * s + 4].astype(F32).reshape(4 * I, D)).astype(BF)


def project(rows, w_ref):
    return jnp.dot(rows, w_ref[...], preferred_element_type=F32).astype(BF)


def own_kernel(x_ref, mate_ref, wq_ref, wk_ref, q_ref, k_ref):
    for s in range(2):
        rows = normed_rows(x_ref, s)
        store_block(q_ref, 0, 4 * s, project(rows, wq_ref))
        store_block(k_ref, 0, 4 * s, project(rows, wk_ref))
        store_block(q_ref, I, 4 * s, project(normed_rows(mate_ref, s), wq_ref))


def near_kernel(key_ref, a_ref, wk_ref, q_ref, out_ref, keys, rows):
    keys[:, :I] = key_ref[...]
    for s in range(2):
        store_block(keys, I, 4 * s, project(normed_rows(a_ref, s), wk_ref))
    store_logits(q_ref, keys, rows, out_ref)


def far_kernel(b_ref, far_ref, wk_ref, q_ref, out_ref, keys, rows):
    for at, ref in ((0, b_ref), (I, far_ref)):
        for s in range(2):
            store_block(keys, at, 4 * s, project(normed_rows(ref, s), wk_ref))
    store_logits(q_ref, keys, rows, out_ref)


def block(*shape):
    return pl.BlockSpec(shape, lambda s: (0,) * len(shape))


def weight(part):
    return pl.BlockSpec((D, D), lambda s: (0, part))


LOGITS = jax.ShapeDtypeStruct((32, 48, 128), BF)
ONE = jax.ShapeDtypeStruct((PAIRS, I, R * 128), BF)
TWO = jax.ShapeDtypeStruct((PAIRS, 2 * I, R * 128), BF)
ROWS = pltpu.VMEM((2, D, 128), F32)
KEYS = pltpu.VMEM((PAIRS, 128, R * 128), BF)


def own_projections(x, mate, w):
    whole, one, two = block(R, I, D), block(*ONE.shape), block(*TWO.shape)
    return pl.pallas_call(
        own_kernel,
        grid=(1,),
        out_shape=(TWO, ONE),
        in_specs=[whole, whole, weight(0), weight(1)],
        out_specs=(two, one),
        compiler_params=params(64 * MB),
        cost_estimate=cost(2.4e9, 9e6),
        name="own_projections",
    )(x, mate, w, w)


def near_logits(keys, a, w, q):
    whole, one, two = block(R, I, D), block(*ONE.shape), block(*TWO.shape)
    return pl.pallas_call(
        near_kernel,
        grid=(1,),
        out_shape=LOGITS,
        in_specs=[one, whole, weight(1), two],
        out_specs=block(32, 48, 128),
        scratch_shapes=[KEYS, ROWS],
        compiler_params=params(64 * MB),
        cost_estimate=cost(3e9, 8e6),
        name="near_logits",
    )(keys, a, w, q)


def far_logits(b, far, w, q):
    whole = block(R, I, D)
    return pl.pallas_call(
        far_kernel,
        grid=(1,),
        out_shape=LOGITS,
        in_specs=[whole, whole, weight(1), block(*TWO.shape)],
        out_specs=block(32, 48, 128),
        scratch_shapes=[KEYS, ROWS],
        compiler_params=params(64 * MB),
        cost_estimate=cost(3e9, 7e6),
        name="far_logits",
    )(b, far, w, q)


HBM = pl.BlockSpec(memory_space=pltpu.HBM)
BLOCKS = 8


def value_kernel(core, *refs):
    block_refs, w_ref = refs[:BLOCKS], refs[BLOCKS]
    out_ref, rows, wv, done, loaded, stored, weighed = refs[-7:]

    @pl.when(lax.axis_index("core") == core)
    def _():
        weights = pltpu.make_async_copy(w_ref.at[:, pl.ds(2 * D, D)], wv, weighed)
        loads, stores = [], []
        for n, ref in enumerate(block_refs):
            slot = n % 2
            loads.append(pltpu.make_async_copy(ref, rows.at[slot], loaded.at[slot]))
            target = out_ref.at[:, pl.ds(n * I, I)]
            stores.append(pltpu.make_async_copy(done.at[slot], target, stored.at[slot]))
        weights.start()
        loads[0].start()
        weights.wait()
        for n in range(BLOCKS):
            slot = n % 2
            if n + 1 < BLOCKS:
                loads[n + 1].start()
            loads[n].wait()
            if n >= 2:
                stores[n - 2].wait()
            for s in range(2):
                store_block(done.at[slot], 0, 4 * s, project(normed_rows(rows.at[slot], s), wv))
            stores[n].start()
        stores[BLOCKS - 2].wait()
        stores[BLOCKS - 1].wait()


def all_values(core, blocks, w, before=None):
    operands = [*blocks, w] + ([] if before is None else [before])
    return pl.pallas_call(
        functools.partial(value_kernel, core),
        out_shape=jax.ShapeDtypeStruct((PAIRS, BLOCKS * I, R * 128), BF),
        in_specs=[HBM] * len(operands),
        out_specs=HBM,
        input_output_aliases={} if before is None else {BLOCKS + 1: 0},
        scratch_shapes=[
            pltpu.VMEM((2, R, I, D), BF),
            pltpu.VMEM((D, D), BF),
            pltpu.VMEM((2, PAIRS, I, R * 128), BF),
            pltpu.SemaphoreType.DMA((2,)),
            pltpu.SemaphoreType.DMA((2,)),
            pltpu.SemaphoreType.DMA,
        ],
        compiler_params=params(64 * MB),
        cost_estimate=cost(5e9, 1.5e7),
        name="values_%d" % core,
    )(*operands)


def sum_kernel(near_ref, far_ref, mine_ref, mates_ref, rows):
    totals = [jnp.sum(ref[...].astype(F32), axis=0) for ref in (near_ref, far_ref)]
    rows[...] = jnp.concatenate(totals, axis=1).reshape(2, 24, 256)
    core = lax.axis_index("core")
    mine_ref[...] = rows[core]
    mates_ref[...] = rows[1 - core]


def sum_logits(near, far):
    return pl.pallas_call(
        sum_kernel,
        out_shape=(jax.ShapeDtypeStruct((24, 256), F32),) * 2,
        in_specs=[VMEM, VMEM],
        out_specs=(VMEM, VMEM),
        scratch_shapes=[pltpu.VMEM((2, 24, 256), F32)],
        compiler_params=params(),
        cost_estimate=cost(1e6, 1e6),
        name="sum_logits",
    )(near, far)


def weight_kernel(scale, copies, near_ref, far_ref, out_ref):
    logits = jnp.concatenate([near_ref[...], far_ref[...]], axis=1)
    top = jnp.max(logits, axis=-1, keepdims=True)
    powers = jnp.exp2((logits - top) * (scale * LOG2E))
    weights = (powers / jnp.sum(powers, axis=-1, keepdims=True)).astype(BF)
    for c in range(copies):
        out_ref[c] = weights


def row_weights(own, mates, scale, copies):
    return pl.pallas_call(
        functools.partial(weight_kernel, scale, copies),
        out_shape=jax.ShapeDtypeStruct((copies, 24, 512), BF),
        in_specs=[VMEM] * 2,
        out_specs=VMEM,
        compiler_params=params(),
        cost_estimate=cost(1e6, 1e6),
        name="row_weights",
    )(own, mates)


def reorder(major, minor):
    n = major * minor
    to = lax.broadcasted_iota(jnp.int32, (n, n), 0)
    at = lax.broadcasted_iota(jnp.int32, (n, n), 1)
    source = lax.rem(to, major) * minor + lax.div(to, major)
    return jnp.where(at == source, 1.0, 0.0).astype(BF)


STEP = 3


def context_kernel(w0, w1, w2, w3, value_ref, x_ref, wo_ref, out_ref, wall, ctx, x_own, wo, sems):
    g = pl.program_id(0)
    late = [
        pltpu.make_async_copy(wo_ref, wo, sems.at[0]),
        pltpu.make_async_copy(x_ref, x_own, sems.at[1]),
    ]

    @pl.when(g == 0)
    def _():
        place = lax.axis_index("x")
        for step, w in enumerate((w0, w1, w2, w3)):
            wall[lax.rem(place + step, 4)] = w[...].reshape(3, I, 512)
        for copy in late:
            copy.start()

    first = first_head(I)
    for n in range(STEP):
        pair = []
        for h in range(2):
            head = (g * STEP + n) * 2 + h
            pair.append(wall[lax.div(head, 3), lax.rem(head, 3)])
        weights = jnp.concatenate(pair, axis=0)
        both = jnp.dot(weights, value_ref[n], preferred_element_type=F32)
        for r in range(R):
            lanes = slice(r * 128, (r + 1) * 128)
            piece = jnp.where(first, both[:I, lanes], both[I:, lanes]).astype(BF)
            ctx[g * STEP + n, r * I : (r + 1) * I, :] = piece

    @pl.when(g == PAIRS // STEP - 1)
    def _():
        for copy in late:
            copy.wait()
        context = jnp.concatenate([ctx[n] for n in range(PAIRS)], axis=1)
        update = jnp.dot(context, wo[...], preferred_element_type=F32)
        after = (x_own[...].astype(F32).reshape(R * I, D) + update).astype(BF)
        out_ref[...] = jnp.dot(reorder(R, I), after, preferred_element_type=F32).astype(BF)


def row_context(weights, values, x, wo):
    whole = pl.BlockSpec((192, 512), lambda p: (0, 0))
    value = pl.BlockSpec((STEP, BLOCKS * I, R * 128), lambda p: (p, 0, 0))
    return pl.pallas_call(
        context_kernel,
        grid=(PAIRS // STEP,),
        out_shape=jax.ShapeDtypeStruct((R * I, D), BF),
        in_specs=[whole] * 4
        + [value, HBM, HBM],
        out_specs=pl.BlockSpec((R * I, D), lambda p: (0, 0)),
        scratch_shapes=[
            pltpu.VMEM((4, 3, I, 512), BF),
            pltpu.VMEM((PAIRS, R * I, 128), BF),
            pltpu.VMEM((R, I, D), BF),
            pltpu.VMEM((D, D), BF),
            pltpu.SemaphoreType.DMA((2,)),
        ],
        compiler_params=params(62 * MB),
        cost_estimate=cost(2e9, 1e7),
        name="row_context",
    )(*weights, values, x, wo)


def column_kernel(x_ref, wq_ref, wk_ref, wv_ref, wo_ref, out_ref, normed, context, wo, sem):
    g = pl.program_id(0)
    late = pltpu.make_async_copy(wo_ref, wo, sem)

    def column(c):
        return x_ref[...].astype(F32).reshape(32, 2, R, D)[:, c].reshape(256, D)

    @pl.when(g == 0)
    def _():
        late.start()
        for c in range(2):
            normed[c * 256 : (c + 1) * 256] = layer_norm(column(c)).astype(BF)

    rows = normed[...]
    q = jnp.dot(rows, wq_ref[...], preferred_element_type=F32).astype(BF)
    k = jnp.dot(rows, wk_ref[...], preferred_element_type=F32).astype(BF)
    v = jnp.dot(rows, wv_ref[...], preferred_element_type=F32).astype(BF)
    first = first_head(256)
    zero = jnp.zeros((256, 128), BF)
    for c in range(2):
        rows = slice(c * 256, (c + 1) * 256)
        for p in range(2):
            at = (rows, slice(p * 128, (p + 1) * 128))
            both = jnp.concatenate(
                [jnp.where(first, q[at], zero), jnp.where(first, zero, q[at])], axis=0
            )
            scores = lax.dot_general(both, k[at], NT, preferred_element_type=F32)
            top = jnp.max(scores, axis=-1, keepdims=True)
            powers = jnp.exp2((scores - top) * (64**-0.5 * LOG2E))
            weight = jnp.sum(powers, axis=-1, keepdims=True)
            mixed = jnp.dot(powers.astype(BF), v[at], preferred_element_type=F32) / weight
            context[2 * g + p, rows] = jnp.where(first, mixed[:256], mixed[256:]).astype(BF)

    @pl.when(g == 2)
    def _():
        late.wait()
        whole = jnp.concatenate([context[p] for p in range(PAIRS)], axis=1)
        update = jnp.dot(whole, wo[...], preferred_element_type=F32)
        both = [(column(c) + update[c * 256 : (c + 1) * 256]).reshape(32, R, D) for c in range(2)]
        out_ref[...] = jnp.concatenate(both, axis=1).astype(BF)


def attend_columns(x, w, wo):
    whole = pl.BlockSpec((32, 2 * R, D), lambda g: (0, 0, 0))
    return pl.pallas_call(
        column_kernel,
        grid=(3,),
        out_shape=jax.ShapeDtypeStruct((32, 2 * R, D), BF),
        in_specs=[
            whole,
            pl.BlockSpec((D, 256), lambda g: (0, g)),
            pl.BlockSpec((D, 256), lambda g: (0, g + 3)),
            pl.BlockSpec((D, 256), lambda g: (0, g + 6)),
            HBM,
        ],
        out_specs=whole,
        scratch_shapes=[
            pltpu.VMEM((512, D), BF),
            pltpu.VMEM((PAIRS, 512, 128), BF),
            pltpu.VMEM((D, D), BF),
            pltpu.SemaphoreType.DMA,
        ],
        compiler_params=params(62 * MB),
        cost_estimate=cost(5e9, 7e6, 1600000),
        name="columns",
    )(x, w, w, w, wo)


def finish_kernel(x_ref, out_ref):
    rows = jnp.dot(reorder(I, R), x_ref[...], preferred_element_type=F32).astype(BF)
    for r in range(R):
        out_ref[r] = rows[r * I : (r + 1) * I]


def finish(x):
    return pl.pallas_call(
        finish_kernel,
        out_shape=jax.ShapeDtypeStruct((R, I, D), BF),
        in_specs=[VMEM],
        out_specs=VMEM,
        compiler_params=params(),
        cost_estimate=cost(4e8, 1.6e6),
        name="finish",
    )(x)


def shift(n, by):
    return [(i, (i + by) % n) for i in range(n)]


def per_device(x, w_row, wo_row, w_col, wo_col):
    exchange = functools.partial(
        lax.all_to_all, axis_name=("x", "z"), split_axis=0, concat_axis=0, tiled=True
    )
    mate = functools.partial(lax.ppermute, axis_name="core", perm=shift(2, 1))
    ways = [[(2 * y + c, 2 * ((y + 1 - 2 * c) % 4) + c) for y in range(4) for c in range(2)]]
    ways.append([(b, a) for a, b in ways[0]])
    on, back = [functools.partial(lax.ppermute, axis_name=("y", "core"), perm=way) for way in ways]
    along = [functools.partial(lax.ppermute, axis_name="x", perm=shift(4, k)) for k in range(4)]

    a, own = on(x), mate(x)
    q, keys = own_projections(x, own, w_row)
    later, q = lax.optimization_barrier((x, q))
    b, far = back(later), on(a)
    near = near_logits(keys, a, w_row, q)
    b, far, _ = lax.optimization_barrier((b, far, near))
    near = exchange(near)
    logits = far_logits(b, far, w_row, q)
    b, far, logits = lax.optimization_barrier((b, far, logits))
    logits, near = lax.optimization_barrier((logits, near))
    blocks = (x, a, b, far, own, mate(a), mate(b), mate(far))
    logits = exchange(logits)
    values = all_values(0, blocks, w_row)
    logits, values = lax.optimization_barrier((logits, values))
    mine, other = sum_logits(near, logits)
    copies = row_weights(mine, mate(other), float((64 * 256) ** -0.5), 8)
    copies, values = lax.optimization_barrier((copies, values))
    values = all_values(1, blocks, w_row, values)
    copies, values = lax.optimization_barrier((copies, values))
    mine = lax.all_to_all(copies, "z", 0, 0, tiled=True).reshape(192, 512)
    weights = [mine] + [along[4 - k](mine) for k in (1, 2, 3)]
    rows = row_context(weights, values, x, wo_row)
    columns = exchange(rows.reshape(32, 2 * R, D))
    columns = attend_columns(columns, w_col, wo_col)
    rows = exchange(columns)
    return finish(rows.reshape(R * I, D))


def solution(mesh):
    chips = Mesh(mesh.devices.reshape(4, 8, 4, 2), ("x", "z", "y", "core"))
    rows = P(("x", "z"), ("y", "core"), None)
    return jax.shard_map(
        per_device, mesh=chips, in_specs=(rows, P(), P(), P(), P()), out_specs=rows, check_vma=False
    )
```

```python
import functools

import jax
import jax.numpy as jnp
from jax import lax
from jax.experimental import pallas as pl
from jax.experimental.pallas import tpu as pltpu
from jax.sharding import Mesh, PartitionSpec as P

HEADS = 12
PAIRS = 6
D = 768
R = 8
I = 64
EPS = 1e-05
LOG2E = 1.4426950408889634
NT = (((1,), (1,)), ((), ()))
BF = jnp.bfloat16
F32 = jnp.float32
VMEM = pl.BlockSpec(memory_space=pltpu.VMEM)
MB = 1024 * 1024


def params(limit=48 * MB):
    return pltpu.CompilerParams(vmem_limit_bytes=limit)


def cost(flops, bytes_accessed, transcendentals=0):
    return pl.CostEstimate(
        flops=int(flops), bytes_accessed=int(bytes_accessed), transcendentals=int(transcendentals)
    )


def layer_norm(x):
    mean = jnp.mean(x, axis=-1, keepdims=True)
    centered = x - mean
    spread = jnp.mean(centered * centered, axis=-1, keepdims=True)
    return centered * lax.rsqrt(spread + EPS)


def first_head(rows):
    return lax.broadcasted_iota(jnp.int32, (rows, 128), 1) < 64


def store_block(ref, at, first, rows):
    for p in range(PAIRS):
        for r in range(rows.shape[0] // I):
            lanes = (first + r) * 128
            piece = rows[r * I : (r + 1) * I, p * 128 : (p + 1) * 128]
            ref[p, at : at + I, lanes : lanes + 128] = piece


def store_logits(q_ref, keys, rows, out_ref):
    first = lax.rem(lax.broadcasted_iota(jnp.int32, (I, R * 128), 1), 128) < 64
    zero = jnp.zeros((I, R * 128), BF)
    core = lax.axis_index("core")
    for p in range(PAIRS):
        masked = []
        for part in range(2):
            q = q_ref[p, part * I : (part + 1) * I]
            masked += [jnp.where(first, q, zero), jnp.where(first, zero, q)]
        logits = lax.dot_general(
            jnp.concatenate(masked, axis=0), keys[p], NT, preferred_element_type=F32
        )
        rows[core, p * 128 : (p + 1) * 128] = logits[:128]
        rows[1 - core, p * 128 : (p + 1) * 128] = logits[128:]
    both = [rows[c].reshape(32, 24, 128) for c in range(2)]
    out_ref[...] = jnp.concatenate(both, axis=1).astype(BF)


def normed_rows(ref, s):
    return layer_norm(ref[4 * s : 4 * s + 4].astype(F32).reshape(4 * I, D)).astype(BF)


def project(rows, w_ref):
    return jnp.dot(rows, w_ref[...], preferred_element_type=F32).astype(BF)


def own_kernel(x_ref, mate_ref, wq_ref, wk_ref, q_ref, k_ref):
    for s in range(2):
        rows = normed_rows(x_ref, s)
        store_block(q_ref, 0, 4 * s, project(rows, wq_ref))
        store_block(k_ref, 0, 4 * s, project(rows, wk_ref))
        store_block(q_ref, I, 4 * s, project(normed_rows(mate_ref, s), wq_ref))


def near_kernel(key_ref, a_ref, wk_ref, q_ref, out_ref, keys, rows):
    keys[:, :I] = key_ref[...]
    for s in range(2):
        store_block(keys, I, 4 * s, project(normed_rows(a_ref, s), wk_ref))
    store_logits(q_ref, keys, rows, out_ref)


def far_kernel(b_ref, far_ref, wk_ref, q_ref, out_ref, keys, rows, q, sem):
    queries = pltpu.make_async_copy(q_ref, q, sem)
    queries.start()
    for at, ref in ((0, b_ref), (I, far_ref)):
        for s in range(2):
            store_block(keys, at, 4 * s, project(normed_rows(ref, s), wk_ref))
    queries.wait()
    store_logits(q, keys, rows, out_ref)


def block(*shape):
    return pl.BlockSpec(shape, lambda s: (0,) * len(shape))


def weight(part):
    return pl.BlockSpec((D, D), lambda s: (0, part))


HBM = pl.BlockSpec(memory_space=pltpu.HBM)
LOGITS = jax.ShapeDtypeStruct((32, 48, 128), BF)
ONE = jax.ShapeDtypeStruct((PAIRS, I, R * 128), BF)
TWO = jax.ShapeDtypeStruct((PAIRS, 2 * I, R * 128), BF)
ROWS = pltpu.VMEM((2, D, 128), F32)
KEYS = pltpu.VMEM((PAIRS, 128, R * 128), BF)


def own_projections(x, mate, w):
    whole, one, two = block(R, I, D), block(*ONE.shape), block(*TWO.shape)
    return pl.pallas_call(
        own_kernel,
        grid=(1,),
        out_shape=(TWO, ONE),
        in_specs=[whole, whole, weight(0), weight(1)],
        out_specs=(two, one),
        compiler_params=params(64 * MB),
        cost_estimate=cost(2.4e9, 9e6),
        name="own_projections",
    )(x, mate, w, w)


def near_logits(keys, a, w, q):
    whole, one, two = block(R, I, D), block(*ONE.shape), block(*TWO.shape)
    return pl.pallas_call(
        near_kernel,
        grid=(1,),
        out_shape=LOGITS,
        in_specs=[one, whole, weight(1), two],
        out_specs=block(32, 48, 128),
        scratch_shapes=[KEYS, ROWS],
        compiler_params=params(64 * MB),
        cost_estimate=cost(3e9, 8e6),
        name="near_logits",
    )(keys, a, w, q)


def far_logits(b, far, w, q):
    whole = block(R, I, D)
    return pl.pallas_call(
        far_kernel,
        grid=(1,),
        out_shape=LOGITS,
        in_specs=[whole, whole, weight(1), HBM],
        out_specs=block(32, 48, 128),
        scratch_shapes=[KEYS, ROWS, KEYS, pltpu.SemaphoreType.DMA],
        compiler_params=params(64 * MB),
        cost_estimate=cost(3e9, 7e6),
        name="far_logits",
    )(b, far, w, q)


BLOCKS = 8


def value_kernel(core, *refs):
    block_refs, w_ref = refs[:BLOCKS], refs[BLOCKS]
    out_ref, rows, wv, done, loaded, stored, weighed = refs[-7:]

    @pl.when(lax.axis_index("core") == core)
    def _():
        weights = pltpu.make_async_copy(w_ref.at[:, pl.ds(2 * D, D)], wv, weighed)
        loads, stores = [], []
        for n, ref in enumerate(block_refs):
            slot = n % 2
            loads.append(pltpu.make_async_copy(ref, rows.at[slot], loaded.at[slot]))
            target = out_ref.at[:, pl.ds(n * I, I)]
            stores.append(pltpu.make_async_copy(done.at[slot], target, stored.at[slot]))
        weights.start()
        loads[0].start()
        weights.wait()
        for n in range(BLOCKS):
            slot = n % 2
            if n + 1 < BLOCKS:
                loads[n + 1].start()
            loads[n].wait()
            if n >= 2:
                stores[n - 2].wait()
            for s in range(2):
                store_block(done.at[slot], 0, 4 * s, project(normed_rows(rows.at[slot], s), wv))
            stores[n].start()
        stores[BLOCKS - 2].wait()
        stores[BLOCKS - 1].wait()


def all_values(core, blocks, w, before=None):
    operands = [*blocks, w] + ([] if before is None else [before])
    return pl.pallas_call(
        functools.partial(value_kernel, core),
        out_shape=jax.ShapeDtypeStruct((PAIRS, BLOCKS * I, R * 128), BF),
        in_specs=[HBM] * len(operands),
        out_specs=HBM,
        input_output_aliases={} if before is None else {BLOCKS + 1: 0},
        scratch_shapes=[
            pltpu.VMEM((2, R, I, D), BF),
            pltpu.VMEM((D, D), BF),
            pltpu.VMEM((2, PAIRS, I, R * 128), BF),
            pltpu.SemaphoreType.DMA((2,)),
            pltpu.SemaphoreType.DMA((2,)),
            pltpu.SemaphoreType.DMA,
        ],
        compiler_params=params(62 * MB if core else 64 * MB),
        cost_estimate=cost(5e9, 1.5e7),
        name="values_%d" % core,
    )(*operands)


def sum_kernel(near_ref, far_ref, mine_ref, mates_ref, rows):
    totals = [jnp.sum(ref[...].astype(F32), axis=0) for ref in (near_ref, far_ref)]
    rows[...] = jnp.concatenate(totals, axis=1).reshape(2, 24, 256)
    core = lax.axis_index("core")
    mine_ref[...] = rows[core]
    mates_ref[...] = rows[1 - core]


def sum_logits(near, far):
    return pl.pallas_call(
        sum_kernel,
        out_shape=(jax.ShapeDtypeStruct((24, 256), F32),) * 2,
        in_specs=[VMEM, VMEM],
        out_specs=(VMEM, VMEM),
        scratch_shapes=[pltpu.VMEM((2, 24, 256), F32)],
        compiler_params=params(),
        cost_estimate=cost(1e6, 1e6),
        name="sum_logits",
    )(near, far)


def weight_kernel(scale, copies, near_ref, far_ref, out_ref):
    logits = jnp.concatenate([near_ref[...], far_ref[...]], axis=1)
    top = jnp.max(logits, axis=-1, keepdims=True)
    powers = jnp.exp2((logits - top) * (scale * LOG2E))
    weights = (powers / jnp.sum(powers, axis=-1, keepdims=True)).astype(BF)
    for c in range(copies):
        out_ref[c] = weights


def row_weights(own, mates, scale, copies):
    return pl.pallas_call(
        functools.partial(weight_kernel, scale, copies),
        out_shape=jax.ShapeDtypeStruct((copies, 24, 512), BF),
        in_specs=[VMEM] * 2,
        out_specs=VMEM,
        compiler_params=params(),
        cost_estimate=cost(1e6, 1e6),
        name="row_weights",
    )(own, mates)


def reorder(major, minor):
    n = major * minor
    to = lax.broadcasted_iota(jnp.int32, (n, n), 0)
    at = lax.broadcasted_iota(jnp.int32, (n, n), 1)
    source = lax.rem(to, major) * minor + lax.div(to, major)
    return jnp.where(at == source, 1.0, 0.0).astype(BF)


STEP = 3


def context_kernel(w0, w1, w2, w3, value_ref, x_ref, wo_ref, out_ref, wall, ctx, x_own, wo, sems):
    g = pl.program_id(0)
    late = [
        pltpu.make_async_copy(wo_ref, wo, sems.at[0]),
        pltpu.make_async_copy(x_ref, x_own, sems.at[1]),
    ]

    @pl.when(g == 0)
    def _():
        place = lax.axis_index("x")
        for step, w in enumerate((w0, w1, w2, w3)):
            wall[lax.rem(place + step, 4)] = w[...].reshape(3, I, 512)
        for copy in late:
            copy.start()

    first = first_head(I)
    for n in range(STEP):
        pair = []
        for h in range(2):
            head = (g * STEP + n) * 2 + h
            pair.append(wall[lax.div(head, 3), lax.rem(head, 3)])
        weights = jnp.concatenate(pair, axis=0)
        both = jnp.dot(weights, value_ref[n], preferred_element_type=F32)
        for r in range(R):
            lanes = slice(r * 128, (r + 1) * 128)
            piece = jnp.where(first, both[:I, lanes], both[I:, lanes]).astype(BF)
            ctx[g * STEP + n, r * I : (r + 1) * I, :] = piece

    @pl.when(g == PAIRS // STEP - 1)
    def _():
        for copy in late:
            copy.wait()
        context = jnp.concatenate([ctx[n] for n in range(PAIRS)], axis=1)
        update = jnp.dot(context, wo[...], preferred_element_type=F32)
        after = (x_own[...].astype(F32).reshape(R * I, D) + update).astype(BF)
        out_ref[...] = jnp.dot(reorder(R, I), after, preferred_element_type=F32).astype(BF)


def row_context(weights, values, x, wo):
    whole = pl.BlockSpec((192, 512), lambda p: (0, 0))
    value = pl.BlockSpec((STEP, BLOCKS * I, R * 128), lambda p: (p, 0, 0))
    return pl.pallas_call(
        context_kernel,
        grid=(PAIRS // STEP,),
        out_shape=jax.ShapeDtypeStruct((R * I, D), BF),
        in_specs=[whole] * 4
        + [value, HBM, HBM],
        out_specs=pl.BlockSpec((R * I, D), lambda p: (0, 0)),
        scratch_shapes=[
            pltpu.VMEM((4, 3, I, 512), BF),
            pltpu.VMEM((PAIRS, R * I, 128), BF),
            pltpu.VMEM((R, I, D), BF),
            pltpu.VMEM((D, D), BF),
            pltpu.SemaphoreType.DMA((2,)),
        ],
        compiler_params=params(62 * MB),
        cost_estimate=cost(2e9, 1e7),
        name="row_context",
    )(*weights, values, x, wo)


def column_kernel(x_ref, wq_ref, wk_ref, wv_ref, wo_ref, out_ref, normed, context, wo, sem):
    g = pl.program_id(0)
    late = pltpu.make_async_copy(wo_ref, wo, sem)

    def column(c):
        return x_ref[...].astype(F32).reshape(32, 2, R, D)[:, c].reshape(256, D)

    @pl.when(g == 0)
    def _():
        late.start()
        for c in range(2):
            normed[c * 256 : (c + 1) * 256] = layer_norm(column(c)).astype(BF)

    rows = normed[...]
    q = jnp.dot(rows, wq_ref[...], preferred_element_type=F32).astype(BF)
    k = jnp.dot(rows, wk_ref[...], preferred_element_type=F32).astype(BF)
    v = jnp.dot(rows, wv_ref[...], preferred_element_type=F32).astype(BF)
    first = first_head(256)
    zero = jnp.zeros((256, 128), BF)
    cells = [(c, p) for c in range(2) for p in range(2)]
    ats = [(slice(c * 256, (c + 1) * 256), slice(p * 128, (p + 1) * 128)) for c, p in cells]
    scores = []
    for at in ats:
        both = jnp.concatenate([jnp.where(first, q[at], zero), jnp.where(first, zero, q[at])], axis=0)
        scores.append(lax.dot_general(both, k[at], NT, preferred_element_type=F32))
    for (c, p), at, score in zip(cells, ats, scores):
        top = jnp.max(score, axis=-1, keepdims=True)
        powers = jnp.exp2((score - top) * (64**-0.5 * LOG2E))
        weight = jnp.sum(powers, axis=-1, keepdims=True)
        mixed = jnp.dot(powers.astype(BF), v[at], preferred_element_type=F32) / weight
        context[2 * g + p, at[0]] = jnp.where(first, mixed[:256], mixed[256:]).astype(BF)

    @pl.when(g == 2)
    def _():
        late.wait()
        whole = jnp.concatenate([context[p] for p in range(PAIRS)], axis=1)
        update = jnp.dot(whole, wo[...], preferred_element_type=F32)
        both = [(column(c) + update[c * 256 : (c + 1) * 256]).reshape(32, R, D) for c in range(2)]
        out_ref[...] = jnp.concatenate(both, axis=1).astype(BF)


def attend_columns(x, w, wo):
    whole = pl.BlockSpec((32, 2 * R, D), lambda g: (0, 0, 0))
    return pl.pallas_call(
        column_kernel,
        grid=(3,),
        out_shape=jax.ShapeDtypeStruct((32, 2 * R, D), BF),
        in_specs=[
            whole,
            pl.BlockSpec((D, 256), lambda g: (0, g)),
            pl.BlockSpec((D, 256), lambda g: (0, g + 3)),
            pl.BlockSpec((D, 256), lambda g: (0, g + 6)),
            HBM,
        ],
        out_specs=whole,
        scratch_shapes=[
            pltpu.VMEM((512, D), BF),
            pltpu.VMEM((PAIRS, 512, 128), BF),
            pltpu.VMEM((D, D), BF),
            pltpu.SemaphoreType.DMA,
        ],
        compiler_params=params(62 * MB),
        cost_estimate=cost(5e9, 7e6, 1600000),
        name="columns",
    )(x, w, w, w, wo)


def finish_kernel(x_ref, out_ref):
    rows = jnp.dot(reorder(I, R), x_ref[...], preferred_element_type=F32).astype(BF)
    for r in range(R):
        out_ref[r] = rows[r * I : (r + 1) * I]


def finish(x):
    return pl.pallas_call(
        finish_kernel,
        out_shape=jax.ShapeDtypeStruct((R, I, D), BF),
        in_specs=[VMEM],
        out_specs=VMEM,
        compiler_params=params(),
        cost_estimate=cost(4e8, 1.6e6),
        name="finish",
    )(x)


def shift(n, by):
    return [(i, (i + by) % n) for i in range(n)]


def per_device(x, w_row, wo_row, w_col, wo_col):
    exchange = functools.partial(
        lax.all_to_all, axis_name=("x", "z"), split_axis=0, concat_axis=0, tiled=True
    )
    mate = functools.partial(lax.ppermute, axis_name="core", perm=shift(2, 1))
    ways = [[(2 * y + c, 2 * ((y + 1 - 2 * c) % 4) + c) for y in range(4) for c in range(2)]]
    ways.append([(b, a) for a, b in ways[0]])
    on, back = [functools.partial(lax.ppermute, axis_name=("y", "core"), perm=way) for way in ways]
    along = [functools.partial(lax.ppermute, axis_name="x", perm=shift(4, k)) for k in range(4)]

    a, own = on(x), mate(x)
    q, keys = own_projections(x, own, w_row)
    later, q = lax.optimization_barrier((x, q))
    b, far = back(later), on(a)
    near = near_logits(keys, a, w_row, q)
    b, far, _ = lax.optimization_barrier((b, far, near))
    near = exchange(near)
    logits = far_logits(b, far, w_row, q)
    b, far, logits = lax.optimization_barrier((b, far, logits))
    logits, near = lax.optimization_barrier((logits, near))
    blocks = (x, a, b, far, own, mate(a), mate(b), mate(far))
    logits = exchange(logits)
    values = all_values(0, blocks, w_row)
    logits, values = lax.optimization_barrier((logits, values))
    mine, other = sum_logits(near, logits)
    copies = row_weights(mine, mate(other), float((64 * 256) ** -0.5), 8)
    copies, values = lax.optimization_barrier((copies, values))
    values = all_values(1, blocks, w_row, values)
    copies, values = lax.optimization_barrier((copies, values))
    mine = lax.all_to_all(copies, "z", 0, 0, tiled=True).reshape(192, 512)
    weights = [mine] + [along[4 - k](mine) for k in (1, 2, 3)]
    rows = row_context(weights, values, x, wo_row)
    columns = exchange(rows.reshape(32, 2 * R, D))
    columns = attend_columns(columns, w_col, wo_col)
    rows = exchange(columns)
    return finish(rows.reshape(R * I, D))


def solution(mesh):
    chips = Mesh(mesh.devices.reshape(4, 8, 4, 2), ("x", "z", "y", "core"))
    rows = P(("x", "z"), ("y", "core"), None)
    return jax.shard_map(
        per_device, mesh=chips, in_specs=(rows, P(), P(), P(), P()), out_specs=rows, check_vma=False
    )
```

```python
import functools

import jax
import jax.numpy as jnp
from jax import lax
from jax.experimental import pallas as pl
from jax.experimental.pallas import tpu as pltpu
from jax.sharding import Mesh, PartitionSpec as P

HEADS = 12
PAIRS = 6
D = 768
R = 8
I = 64
EPS = 1e-05
LOG2E = 1.4426950408889634
NT = (((1,), (1,)), ((), ()))
BF = jnp.bfloat16
F32 = jnp.float32
VMEM = pl.BlockSpec(memory_space=pltpu.VMEM)
MB = 1024 * 1024


def params(limit=48 * MB):
    return pltpu.CompilerParams(vmem_limit_bytes=limit)


def cost(flops, bytes_accessed, transcendentals=0):
    return pl.CostEstimate(
        flops=int(flops), bytes_accessed=int(bytes_accessed), transcendentals=int(transcendentals)
    )


def layer_norm(x):
    mean = jnp.mean(x, axis=-1, keepdims=True)
    centered = x - mean
    spread = jnp.mean(centered * centered, axis=-1, keepdims=True)
    return centered * lax.rsqrt(spread + EPS)


def first_head(rows):
    return lax.broadcasted_iota(jnp.int32, (rows, 128), 1) < 64


def store_block(ref, at, first, rows):
    for p in range(PAIRS):
        for r in range(rows.shape[0] // I):
            lanes = (first + r) * 128
            piece = rows[r * I : (r + 1) * I, p * 128 : (p + 1) * 128]
            ref[p, at : at + I, lanes : lanes + 128] = piece


def store_logits(q_ref, keys, rows, out_ref):
    first = lax.rem(lax.broadcasted_iota(jnp.int32, (I, R * 128), 1), 128) < 64
    zero = jnp.zeros((I, R * 128), BF)
    core = lax.axis_index("core")
    for p in range(PAIRS):
        masked = []
        for part in range(2):
            q = q_ref[p, part * I : (part + 1) * I]
            masked += [jnp.where(first, q, zero), jnp.where(first, zero, q)]
        logits = lax.dot_general(
            jnp.concatenate(masked, axis=0), keys[p], NT, preferred_element_type=F32
        )
        rows[core, p * 128 : (p + 1) * 128] = logits[:128]
        rows[1 - core, p * 128 : (p + 1) * 128] = logits[128:]
    both = [rows[c].reshape(32, 24, 128) for c in range(2)]
    out_ref[...] = jnp.concatenate(both, axis=1).astype(BF)


def normed_rows(ref, s):
    return layer_norm(ref[4 * s : 4 * s + 4].astype(F32).reshape(4 * I, D)).astype(BF)


def project(rows, w_ref):
    return jnp.dot(rows, w_ref[...], preferred_element_type=F32).astype(BF)


def own_kernel(x_ref, mate_ref, wq_ref, wk_ref, q_ref, k_ref):
    for s in range(2):
        rows = normed_rows(x_ref, s)
        store_block(q_ref, 0, 4 * s, project(rows, wq_ref))
        store_block(k_ref, 0, 4 * s, project(rows, wk_ref))
        store_block(q_ref, I, 4 * s, project(normed_rows(mate_ref, s), wq_ref))


def near_kernel(key_ref, a_ref, wk_ref, q_ref, out_ref, keys, rows):
    keys[:, :I] = key_ref[...]
    for s in range(2):
        store_block(keys, I, 4 * s, project(normed_rows(a_ref, s), wk_ref))
    store_logits(q_ref, keys, rows, out_ref)


def far_kernel(b_ref, far_ref, wk_ref, q_ref, out_ref, keys, rows, q, sem):
    queries = pltpu.make_async_copy(q_ref, q, sem)
    queries.start()
    for at, ref in ((0, b_ref), (I, far_ref)):
        for s in range(2):
            store_block(keys, at, 4 * s, project(normed_rows(ref, s), wk_ref))
    queries.wait()
    store_logits(q, keys, rows, out_ref)


def block(*shape):
    return pl.BlockSpec(shape, lambda s: (0,) * len(shape))


def weight(part):
    return pl.BlockSpec((D, D), lambda s: (0, part))


HBM = pl.BlockSpec(memory_space=pltpu.HBM)
LOGITS = jax.ShapeDtypeStruct((32, 48, 128), BF)
ONE = jax.ShapeDtypeStruct((PAIRS, I, R * 128), BF)
TWO = jax.ShapeDtypeStruct((PAIRS, 2 * I, R * 128), BF)
ROWS = pltpu.VMEM((2, D, 128), F32)
KEYS = pltpu.VMEM((PAIRS, 128, R * 128), BF)


def own_projections(x, mate, w):
    whole, one, two = block(R, I, D), block(*ONE.shape), block(*TWO.shape)
    return pl.pallas_call(
        own_kernel,
        grid=(1,),
        out_shape=(TWO, ONE),
        in_specs=[whole, whole, weight(0), weight(1)],
        out_specs=(two, one),
        compiler_params=params(64 * MB),
        cost_estimate=cost(2.4e9, 9e6),
        name="own_projections",
    )(x, mate, w, w)


def near_logits(keys, a, w, q):
    whole, one, two = block(R, I, D), block(*ONE.shape), block(*TWO.shape)
    return pl.pallas_call(
        near_kernel,
        grid=(1,),
        out_shape=LOGITS,
        in_specs=[one, whole, weight(1), two],
        out_specs=block(32, 48, 128),
        scratch_shapes=[KEYS, ROWS],
        compiler_params=params(64 * MB),
        cost_estimate=cost(3e9, 8e6),
        name="near_logits",
    )(keys, a, w, q)


def far_logits(b, far, w, q):
    whole = block(R, I, D)
    return pl.pallas_call(
        far_kernel,
        grid=(1,),
        out_shape=LOGITS,
        in_specs=[whole, whole, weight(1), HBM],
        out_specs=block(32, 48, 128),
        scratch_shapes=[KEYS, ROWS, KEYS, pltpu.SemaphoreType.DMA],
        compiler_params=params(64 * MB),
        cost_estimate=cost(3e9, 7e6),
        name="far_logits",
    )(b, far, w, q)


BLOCKS = 8


def value_kernel(core, places, *refs):
    count = len(places)
    block_refs, w_ref = refs[:count], refs[count]
    out_ref, rows, wv, done, loaded, stored, weighed = refs[-7:]

    @pl.when(lax.axis_index("core") == core)
    def _():
        weights = pltpu.make_async_copy(w_ref.at[:, pl.ds(2 * D, D)], wv, weighed)
        loads, stores = [], []
        for n, ref in enumerate(block_refs):
            slot = n % 2
            loads.append(pltpu.make_async_copy(ref, rows.at[slot], loaded.at[slot]))
            target = out_ref.at[:, pl.ds(places[n] * I, I)]
            stores.append(pltpu.make_async_copy(done.at[slot], target, stored.at[slot]))
        weights.start()
        loads[0].start()
        weights.wait()
        for n in range(count):
            slot = n % 2
            if n + 1 < count:
                loads[n + 1].start()
            loads[n].wait()
            if n >= 2:
                stores[n - 2].wait()
            for s in range(2):
                store_block(done.at[slot], 0, 4 * s, project(normed_rows(rows.at[slot], s), wv))
            stores[n].start()
        stores[count - 2].wait()
        stores[count - 1].wait()


def all_values(core, places, blocks, w, before=None):
    operands = [*blocks, w] + ([] if before is None else [before])
    return pl.pallas_call(
        functools.partial(value_kernel, core, places),
        out_shape=jax.ShapeDtypeStruct((PAIRS, BLOCKS * I, R * 128), BF),
        in_specs=[HBM] * len(operands),
        out_specs=HBM,
        input_output_aliases={} if before is None else {len(places) + 1: 0},
        scratch_shapes=[
            pltpu.VMEM((2, R, I, D), BF),
            pltpu.VMEM((D, D), BF),
            pltpu.VMEM((2, PAIRS, I, R * 128), BF),
            pltpu.SemaphoreType.DMA((2,)),
            pltpu.SemaphoreType.DMA((2,)),
            pltpu.SemaphoreType.DMA,
        ],
        compiler_params=params(62 * MB if core else 64 * MB),
        cost_estimate=cost(5e9, 1.5e7),
        name="values_%d_%d" % (core, len(places)),
    )(*operands)


def sum_kernel(near_ref, far_ref, mine_ref, mates_ref, rows):
    totals = [jnp.sum(ref[...].astype(F32), axis=0) for ref in (near_ref, far_ref)]
    rows[...] = jnp.concatenate(totals, axis=1).reshape(2, 24, 256)
    core = lax.axis_index("core")
    mine_ref[...] = rows[core]
    mates_ref[...] = rows[1 - core]


def sum_logits(near, far):
    return pl.pallas_call(
        sum_kernel,
        out_shape=(jax.ShapeDtypeStruct((24, 256), F32),) * 2,
        in_specs=[VMEM, VMEM],
        out_specs=(VMEM, VMEM),
        scratch_shapes=[pltpu.VMEM((2, 24, 256), F32)],
        compiler_params=params(),
        cost_estimate=cost(1e6, 1e6),
        name="sum_logits",
    )(near, far)


def weight_kernel(scale, copies, near_ref, far_ref, out_ref):
    logits = jnp.concatenate([near_ref[...], far_ref[...]], axis=1)
    top = jnp.max(logits, axis=-1, keepdims=True)
    powers = jnp.exp2((logits - top) * (scale * LOG2E))
    weights = (powers / jnp.sum(powers, axis=-1, keepdims=True)).astype(BF)
    for c in range(copies):
        out_ref[c] = weights


def row_weights(own, mates, scale, copies):
    return pl.pallas_call(
        functools.partial(weight_kernel, scale, copies),
        out_shape=jax.ShapeDtypeStruct((copies, 24, 512), BF),
        in_specs=[VMEM] * 2,
        out_specs=VMEM,
        compiler_params=params(),
        cost_estimate=cost(1e6, 1e6),
        name="row_weights",
    )(own, mates)


def reorder(major, minor):
    n = major * minor
    to = lax.broadcasted_iota(jnp.int32, (n, n), 0)
    at = lax.broadcasted_iota(jnp.int32, (n, n), 1)
    source = lax.rem(to, major) * minor + lax.div(to, major)
    return jnp.where(at == source, 1.0, 0.0).astype(BF)


STEP = 3


def context_kernel(w0, w1, w2, w3, value_ref, x_ref, wo_ref, out_ref, wall, ctx, x_own, wo, sems):
    g = pl.program_id(0)
    late = [
        pltpu.make_async_copy(wo_ref, wo, sems.at[0]),
        pltpu.make_async_copy(x_ref, x_own, sems.at[1]),
    ]

    @pl.when(g == 0)
    def _():
        place = lax.axis_index("x")
        for step, w in enumerate((w0, w1, w2, w3)):
            wall[lax.rem(place + step, 4)] = w[...].reshape(3, I, 512)
        for copy in late:
            copy.start()

    first = first_head(I)
    for n in range(STEP):
        pair = []
        for h in range(2):
            head = (g * STEP + n) * 2 + h
            pair.append(wall[lax.div(head, 3), lax.rem(head, 3)])
        weights = jnp.concatenate(pair, axis=0)
        both = jnp.dot(weights, value_ref[n], preferred_element_type=F32)
        for r in range(R):
            lanes = slice(r * 128, (r + 1) * 128)
            piece = jnp.where(first, both[:I, lanes], both[I:, lanes]).astype(BF)
            ctx[g * STEP + n, r * I : (r + 1) * I, :] = piece

    @pl.when(g == PAIRS // STEP - 1)
    def _():
        for copy in late:
            copy.wait()
        context = jnp.concatenate([ctx[n] for n in range(PAIRS)], axis=1)
        update = jnp.dot(context, wo[...], preferred_element_type=F32)
        after = (x_own[...].astype(F32).reshape(R * I, D) + update).astype(BF)
        out_ref[...] = jnp.dot(reorder(R, I), after, preferred_element_type=F32).astype(BF)


def row_context(weights, values, x, wo):
    whole = pl.BlockSpec((192, 512), lambda p: (0, 0))
    value = pl.BlockSpec((STEP, BLOCKS * I, R * 128), lambda p: (p, 0, 0))
    return pl.pallas_call(
        context_kernel,
        grid=(PAIRS // STEP,),
        out_shape=jax.ShapeDtypeStruct((R * I, D), BF),
        in_specs=[whole] * 4
        + [value, HBM, HBM],
        out_specs=pl.BlockSpec((R * I, D), lambda p: (0, 0)),
        scratch_shapes=[
            pltpu.VMEM((4, 3, I, 512), BF),
            pltpu.VMEM((PAIRS, R * I, 128), BF),
            pltpu.VMEM((R, I, D), BF),
            pltpu.VMEM((D, D), BF),
            pltpu.SemaphoreType.DMA((2,)),
        ],
        compiler_params=params(62 * MB),
        cost_estimate=cost(2e9, 1e7),
        name="row_context",
    )(*weights, values, x, wo)


def column_kernel(x_ref, wq_ref, wk_ref, wv_ref, wo_ref, out_ref, normed, context, wo, sem):
    g = pl.program_id(0)
    late = pltpu.make_async_copy(wo_ref, wo, sem)

    def column(c):
        return x_ref[...].astype(F32).reshape(32, 2, R, D)[:, c].reshape(256, D)

    @pl.when(g == 0)
    def _():
        late.start()
        for c in range(2):
            normed[c * 256 : (c + 1) * 256] = layer_norm(column(c)).astype(BF)

    rows = normed[...]
    q = jnp.dot(rows, wq_ref[...], preferred_element_type=F32).astype(BF)
    k = jnp.dot(rows, wk_ref[...], preferred_element_type=F32).astype(BF)
    v = jnp.dot(rows, wv_ref[...], preferred_element_type=F32).astype(BF)
    first = first_head(256)
    zero = jnp.zeros((256, 128), BF)
    cells = [(c, p) for c in range(2) for p in range(2)]
    ats = [(slice(c * 256, (c + 1) * 256), slice(p * 128, (p + 1) * 128)) for c, p in cells]
    scores = []
    for at in ats:
        both = jnp.concatenate([jnp.where(first, q[at], zero), jnp.where(first, zero, q[at])], axis=0)
        scores.append(lax.dot_general(both, k[at], NT, preferred_element_type=F32))
    for (c, p), at, score in zip(cells, ats, scores):
        top = jnp.max(score, axis=-1, keepdims=True)
        powers = jnp.exp2((score - top) * (64**-0.5 * LOG2E))
        weight = jnp.sum(powers, axis=-1, keepdims=True)
        mixed = jnp.dot(powers.astype(BF), v[at], preferred_element_type=F32) / weight
        context[2 * g + p, at[0]] = jnp.where(first, mixed[:256], mixed[256:]).astype(BF)

    @pl.when(g == 2)
    def _():
        late.wait()
        whole = jnp.concatenate([context[p] for p in range(PAIRS)], axis=1)
        update = jnp.dot(whole, wo[...], preferred_element_type=F32)
        both = [(column(c) + update[c * 256 : (c + 1) * 256]).reshape(32, R, D) for c in range(2)]
        out_ref[...] = jnp.concatenate(both, axis=1).astype(BF)


def attend_columns(x, w, wo):
    whole = pl.BlockSpec((32, 2 * R, D), lambda g: (0, 0, 0))
    return pl.pallas_call(
        column_kernel,
        grid=(3,),
        out_shape=jax.ShapeDtypeStruct((32, 2 * R, D), BF),
        in_specs=[
            whole,
            pl.BlockSpec((D, 256), lambda g: (0, g)),
            pl.BlockSpec((D, 256), lambda g: (0, g + 3)),
            pl.BlockSpec((D, 256), lambda g: (0, g + 6)),
            HBM,
        ],
        out_specs=whole,
        scratch_shapes=[
            pltpu.VMEM((512, D), BF),
            pltpu.VMEM((PAIRS, 512, 128), BF),
            pltpu.VMEM((D, D), BF),
            pltpu.SemaphoreType.DMA,
        ],
        compiler_params=params(62 * MB),
        cost_estimate=cost(5e9, 7e6, 1600000),
        name="columns",
    )(x, w, w, w, wo)


def finish_kernel(x_ref, out_ref):
    rows = jnp.dot(reorder(I, R), x_ref[...], preferred_element_type=F32).astype(BF)
    for r in range(R):
        out_ref[r] = rows[r * I : (r + 1) * I]


def finish(x):
    return pl.pallas_call(
        finish_kernel,
        out_shape=jax.ShapeDtypeStruct((R, I, D), BF),
        in_specs=[VMEM],
        out_specs=VMEM,
        compiler_params=params(),
        cost_estimate=cost(4e8, 1.6e6),
        name="finish",
    )(x)


def shift(n, by):
    return [(i, (i + by) % n) for i in range(n)]


def per_device(x, w_row, wo_row, w_col, wo_col):
    exchange = functools.partial(
        lax.all_to_all, axis_name=("x", "z"), split_axis=0, concat_axis=0, tiled=True
    )
    mate = functools.partial(lax.ppermute, axis_name="core", perm=shift(2, 1))
    ways = [[(2 * y + c, 2 * ((y + 1 - 2 * c) % 4) + c) for y in range(4) for c in range(2)]]
    ways.append([(b, a) for a, b in ways[0]])
    on, back = [functools.partial(lax.ppermute, axis_name=("y", "core"), perm=way) for way in ways]
    along = [functools.partial(lax.ppermute, axis_name="x", perm=shift(4, k)) for k in range(4)]

    a, own = on(x), mate(x)
    q, keys = own_projections(x, own, w_row)
    later, q = lax.optimization_barrier((x, q))
    values = all_values(0, (0, 4), (x, own), w_row)
    a, values = lax.optimization_barrier((a, values))
    b, far = back(later), on(a)
    near = near_logits(keys, a, w_row, q)
    b, far, _ = lax.optimization_barrier((b, far, near))
    near = exchange(near)
    logits = far_logits(b, far, w_row, q)
    b, far, logits = lax.optimization_barrier((b, far, logits))
    logits, near = lax.optimization_barrier((logits, near))
    blocks = (x, a, b, far, own, mate(a), mate(b), mate(far))
    logits = exchange(logits)
    others = [blocks[n] for n in (1, 2, 3, 5, 6, 7)]
    values = all_values(0, (1, 2, 3, 5, 6, 7), others, w_row, values)
    logits, values = lax.optimization_barrier((logits, values))
    mine, other = sum_logits(near, logits)
    copies = row_weights(mine, mate(other), float((64 * 256) ** -0.5), 8)
    copies, values = lax.optimization_barrier((copies, values))
    values = all_values(1, tuple(range(BLOCKS)), blocks, w_row, values)
    copies, values = lax.optimization_barrier((copies, values))
    mine = lax.all_to_all(copies, "z", 0, 0, tiled=True).reshape(192, 512)
    weights = [mine] + [along[4 - k](mine) for k in (1, 2, 3)]
    rows = row_context(weights, values, x, wo_row)
    columns = exchange(rows.reshape(32, 2 * R, D))
    columns = attend_columns(columns, w_col, wo_col)
    rows = exchange(columns)
    return finish(rows.reshape(R * I, D))


def solution(mesh):
    chips = Mesh(mesh.devices.reshape(4, 8, 4, 2), ("x", "z", "y", "core"))
    rows = P(("x", "z"), ("y", "core"), None)
    return jax.shard_map(
        per_device, mesh=chips, in_specs=(rows, P(), P(), P(), P()), out_specs=rows, check_vma=False
    )
```
